32 devices in a mesh: edp: 4 (over z), ep: 8 (over y, x, core).
Axes of the slice: x: 2, y: 2, z: 4, core: 2. Of those that a mesh axis runs over, the one named last changes fastest.
Arguments:
- token_acts: bfloat16 [4, 8, 2, 64, 1024], P('edp', 'ep'), may hold values from -6 to 6
- out_grad: bfloat16 [4, 8, 3584, 128], P('edp', 'ep'), may hold values from -0.59765625 to 0.59765625
- counts: int32 [4, 8, 2], P('edp', 'ep'), may hold values from 1 to 64, as said below
- params: float32 [8, 3584, 1024], P('ep', 'edp'), may hold values from -3 to 3
- first_moment: bfloat16 [8, 3584, 1024], P('ep', 'edp'), may hold values from -3 to 3
- second_moment: bfloat16 [8, 3584, 1024], P('ep', 'edp'), may hold values from 0.049804688 to 2
- old_expert: int32 [8], replicated, may hold values from 0 to 7, each once
- replica_of: int32 [8], replicated, may hold values from 0 to 7
- new_expert: int32 [8], replicated, may hold values from 0 to 7, each once
Outputs:
- update_step: float32 [8, 3584, 1024], P('ep', 'edp')
- new_first: bfloat16 [8, 3584, 1024], P('ep', 'edp')
- new_second: bfloat16 [8, 3584, 1024], P('ep', 'edp')
The draws below stay inside these ranges and needn't reach their ends.
Inputs may be any that keep to these rules, and one draw needn't show every extreme that they name: `counts`: every slot has at least one live token; some slot is full and some slot has exactly one live token in every draw. `old_expert`: each expert appears exactly once. `new_expert`: each expert appears exactly once. `replica_of`: any expert may be served by any number of replica slots, its owner's included.
All inputs are finite; a program needn't handle non-finite values.
Results may differ from the reference program's by a relative error of at most 0.015.
Values may be sent and summed in bfloat16 or wider, within the bound.
No kernel may reach another device: no remote copies, remote signals or barrier semaphores. Data moves between devices by JAX's collectives and lax.ppermute only.
A program may use at most 128 MiB of HBM per device.

```python
import math
import jax
import jax.numpy as jnp
import numpy as np
from jax import lax

D = 3584
FF = 1024
TOK = 64
SLOTS = 2
GROUPS = 4
EXPERTS = 8


def draw_counts(key, part):
    total = GROUPS * EXPERTS * SLOTS
    key_base = jax.random.fold_in(key, 11)
    key_full = jax.random.fold_in(key, 12)
    key_single = jax.random.fold_in(key, 13)
    base = jax.random.randint(key_base, (total,), 1, TOK + 1, dtype=jnp.int32)
    full_at = jax.random.randint(key_full, (), 0, total, dtype=jnp.int32)
    offset = jax.random.randint(key_single, (), 1, total, dtype=jnp.int32)
    single_at = (full_at + offset) % total
    index = jnp.arange(total, dtype=jnp.int32)
    filled = jnp.where(index == full_at, TOK, base)
    filled = jnp.where(index == single_at, 1, filled)
    return filled.reshape(GROUPS, EXPERTS, SLOTS).astype(jnp.int32)


def plant(entries, own_key, low, top_value):
    extent = entries.shape
    index_at = [jax.random.randint(jax.random.fold_in(own_key, axis), (), 0, extent[axis]) for axis in range(len(extent))]
    entries = entries.at[tuple(index_at)].set(low)
    longest = extent.index(max(extent))
    index_at[longest] = (index_at[longest] + 1) % extent[longest]
    return entries.at[tuple(index_at)].set(top_value)


def levels(rng, dims, cuts, least, top_value):
    factor_of = 1.0
    for axis_at, blocks in cuts:
        draws = jax.random.uniform(jax.random.fold_in(jax.random.fold_in(rng, 6), axis_at), (blocks,), jnp.float32, least / len(cuts), top_value / len(cuts))
        factor_of = factor_of * jnp.repeat(jnp.exp(draws), dims[axis_at] // blocks).reshape((-1,) + (1,) * (len(dims) - 1 - axis_at))
    return factor_of


def rank_bounds(amount, skew):
    portions = [(1 << 20) // math.isqrt(rank ** skew) + 1 for rank in range(1, amount + 1)]
    spread = 1 + sum(portions) // (1 << 30)
    return np.cumsum(np.array([max(1, weight // spread) for weight in portions]))


def ranked_ids(own_key, extent, count, skew):
    grid = rank_bounds(count, skew)
    pick = jax.random.randint(jax.random.fold_in(own_key, 1), extent, 0, int(grid[count - 1]))
    rank = jnp.searchsorted(jnp.asarray(grid, jnp.int32), pick, side="right")
    return jax.random.permutation(jax.random.fold_in(own_key, 2), count)[rank].astype(jnp.int32)


def noise(rng, shape, spread, bound, shards=(), kind=jnp.bfloat16):
    array = spread * jax.random.normal(rng, shape, jnp.float32)
    if shards:
        array = array * levels(rng, shape, shards, -0.22, 0.18)
    return jnp.clip(array, -bound, bound).astype(kind)


def setup_inputs(seed: int = 0) -> dict:
    key_of = jax.random.split(jax.random.key(seed), 10)
    return {
        "token_acts": noise(key_of[0], (GROUPS, EXPERTS, SLOTS, TOK, FF), 1.0, 6.0, ((0, 4), (1, 8))),
        "out_grad": noise(key_of[1], (GROUPS, EXPERTS, D, SLOTS * TOK), 0.1, 0.59765625, ((0, 4), (1, 8))),
        "counts": draw_counts(jax.random.fold_in(key_of[9], 71), 0),
        "params": noise(key_of[3], (EXPERTS, D, FF), 0.5, 3.0, ((0, 8), (1, 4)), jnp.float32),
        "first_moment": noise(key_of[4], (EXPERTS, D, FF), 0.5, 3.0, ((0, 8), (1, 4))),
        "second_moment": jnp.clip(jnp.exp(math.log(2.0) - 3.6927934 * jax.random.uniform(key_of[5], (EXPERTS, D, FF), jnp.float32) ** levels(key_of[5], (EXPERTS, D, FF), ((0, 8), (1, 4)), -0.2, 0.2)), 0.049804688, 2.0).astype(jnp.bfloat16),
        "old_expert": jax.random.permutation(key_of[6], EXPERTS).astype(jnp.int32),
        "replica_of": plant(ranked_ids(key_of[7], (EXPERTS,), EXPERTS, 2), jax.random.fold_in(key_of[7], 3), 0, EXPERTS - 1).astype(jnp.int32),
        "new_expert": jax.random.permutation(key_of[8], EXPERTS).astype(jnp.int32),
    }


beta_one = 0.9
beta_two = 0.95
bias_one = 0.9999734386011124
bias_two = 0.994079470779666
decay_rate = 0.1
adam_eps = 1e-08

def adam_update(weights, first_old, second_old, gradient):
    first_new = beta_one * first_old.astype(jnp.float32) + (1.0 - beta_one) * gradient
    second_new = beta_two * second_old.astype(jnp.float32) + (1.0 - beta_two) * gradient * gradient
    scaled = first_new / bias_one / (jnp.sqrt(second_new / bias_two) + adam_eps)
    step_new = -(scaled + decay_rate * weights)
    return (step_new, first_new.astype(jnp.bfloat16), second_new.astype(jnp.bfloat16))

def reference(token_acts, out_grad, counts, params, first_moment, second_moment, old_expert, replica_of, new_expert):
    column = jnp.arange(SLOTS * TOK, dtype=jnp.int32)
    position = column % TOK
    slot_index = column // TOK
    live_limit = counts[:, :, slot_index]
    live_mask = position[None, None, :] < live_limit
    live_grad = jnp.where(live_mask[:, :, None, :], out_grad, jnp.zeros_like(out_grad))

    def slot_grads(expert_index):
        grad_block = live_grad[:, expert_index].astype(jnp.float32).reshape(GROUPS, D, SLOTS, TOK)
        acts_block = token_acts[:, expert_index].astype(jnp.float32)
        return jnp.einsum('gdst,gstf->sdf', grad_block, acts_block, precision=lax.Precision.HIGHEST)
    all_grads = lax.map(slot_grads, jnp.arange(EXPERTS, dtype=jnp.int32))
    own_grad = all_grads[:, 0]
    replica_grad = all_grads[:, 1]
    sum_matrix = (replica_of[None, :] == old_expert[:, None]).astype(jnp.float32)
    summed_grad = own_grad + jnp.einsum('st,tdf->sdf', sum_matrix, replica_grad, precision=lax.Precision.HIGHEST)
    step_new, first_new, second_new = adam_update(params, first_moment, second_moment, summed_grad)
    inverse = jnp.zeros((EXPERTS,), jnp.int32).at[old_expert].set(jnp.arange(EXPERTS, dtype=jnp.int32))
    source = inverse[new_expert]
    return (jnp.take(step_new, source, axis=0), jnp.take(first_new, source, axis=0), jnp.take(second_new, source, axis=0))
```

```python
import functools

import jax
import jax.numpy as jnp
from jax import lax
from jax.experimental import pallas as pl
from jax.experimental.pallas import tpu as pltpu
from jax.sharding import PartitionSpec as P

beta_one = 0.9
beta_two = 0.95
bias_one = 0.9999734386011124
bias_two = 0.994079470779666
decay_rate = 0.1
adam_eps = 1e-08

BF = jnp.bfloat16
F32 = jnp.float32
CHUNK = 16
LIMIT = 56 * 1024 * 1024


def adam_update(weights, first_old, second_old, gradient):
    first_new = beta_one * first_old.astype(F32) + (1.0 - beta_one) * gradient
    second_new = beta_two * second_old.astype(F32) + (1.0 - beta_two) * gradient * gradient
    scaled = first_new / bias_one / (jnp.sqrt(second_new / bias_two) + adam_eps)
    step_new = -(scaled + decay_rate * weights)
    return step_new, first_new, second_new


def mask_kernel(counts, acts, out):
    slots, tok, _ = acts.shape
    row = lax.broadcasted_iota(jnp.int32, (tok, 1), 0)
    for s in range(slots):
        out[s] = jnp.where(row < counts[s], acts[s], jnp.zeros_like(acts[s]))


def pack_kernel(me, params, first, second, *outs):
    at = pl.program_id(0)
    for j, out in enumerate(outs):

        @pl.when(at == j)
        def _(out=out):
            out[0] = params[...].astype(BF)
            out[1] = first[...]
            out[2] = second[...]


def grad_kernel(me, grads, acts, *refs):
    outs, table = refs[:-1], refs[-1]
    at = pl.program_id(0)
    groups, slots, tok, hidden = acts.shape

    @pl.when(at == 0)
    def _():
        zero = jnp.zeros((tok, hidden), BF)
        for g in range(groups):
            for t in range(slots):
                for s in range(slots):
                    rows = pl.ds((g * slots + t) * tok, tok)
                    table[rows, pl.ds(s * hidden, hidden)] = acts[g, s] if s == t else zero

    left = jnp.concatenate([grads[g] for g in range(groups)], axis=1)
    total = jnp.dot(left, table[...], preferred_element_type=F32).astype(BF)
    for j, out in enumerate(outs):

        @pl.when(at == j)
        def _(out=out):
            for s in range(slots):
                out[s] = total[:, s * hidden : (s + 1) * hidden]


def update_kernel(n, me_ref, old, rep, new, *refs):
    params, first, second = refs[:3]
    state = refs[3 : 3 + n - 1]
    grads = refs[2 + n : 2 + 2 * n]
    outs = refs[2 + 2 * n : 2 + 3 * n]
    sums, placed, owner, target = refs[2 + 3 * n :]
    me = me_ref[0]
    for e in range(n):
        owner[old[e]] = e
        target[new[e]] = e
    for k in range(n):
        sums[k] = grads[k][0].astype(F32)
    for k in range(n):
        at = me ^ owner[rep[me ^ k]]
        sums[at] = sums[at] + grads[k][1].astype(F32)
    for k in range(n):
        if k == 0:
            old_state = (params[...], first[...], second[...])
        else:
            old_state = (state[k - 1][0].astype(F32), state[k - 1][1], state[k - 1][2])
        step_new, first_new, second_new = adam_update(*old_state, sums[k])
        to = me ^ target[old[me ^ k]]
        placed[to, 0] = step_new.astype(BF)
        placed[to, 1] = first_new.astype(BF)
        placed[to, 2] = second_new.astype(BF)
    for k in range(n):
        outs[k][...] = placed[k]


def unpack_kernel(me, *refs):
    pieces, (step, first, second) = refs[:-3], refs[-3:]
    at = pl.program_id(0)
    for j, piece in enumerate(pieces):

        @pl.when(at == j)
        def _(piece=piece):
            step[...] = piece[0].astype(F32)
            first[...] = piece[1]
            second[...] = piece[2]


def call(kernel, prefetch, grid, in_specs, out_specs, out_shape, scratch=()):
    return pl.pallas_call(
        kernel,
        grid_spec=pltpu.PrefetchScalarGridSpec(
            num_scalar_prefetch=prefetch,
            grid=grid,
            in_specs=in_specs,
            out_specs=out_specs,
            scratch_shapes=scratch,
        ),
        out_shape=out_shape,
        compiler_params=pltpu.CompilerParams(vmem_limit_bytes=LIMIT),
    )


def swap(array, k, n):
    return lax.ppermute(array, "ep", [(i, i ^ k) for i in range(n)])


def fast_local(
    token_acts, out_grad, counts, params, first_moment, second_moment, old_expert, replica_of, new_expert
):
    groups = lax.axis_size("edp")
    n = lax.axis_size("ep")
    model_width, columns = out_grad.shape[2:]
    slots, tok, hidden = token_acts.shape[2:]
    rows = model_width // groups
    piece = rows // n
    me = lax.axis_index("ep").astype(jnp.int32).reshape(1)
    params, first, second = params[0], first_moment[0], second_moment[0]
    whole = lambda *shape: pl.BlockSpec(shape, lambda i, *_: (0,) * len(shape))

    by_k = lambda i, me: (me[0] ^ (i + 1), 0)
    packed = call(
        pack_kernel,
        1,
        (n - 1,),
        [pl.BlockSpec((piece, hidden), by_k)] * 3,
        [whole(3, piece, hidden)] * (n - 1),
        [jax.ShapeDtypeStruct((3, piece, hidden), BF)] * (n - 1),
    )(me, params, first, second)
    state = [swap(packed[k - 1], k, n) for k in range(1, n)]

    acts = call(
        mask_kernel,
        1,
        (1,),
        [whole(slots, tok, hidden)],
        whole(slots, tok, hidden),
        jax.ShapeDtypeStruct((slots, tok, hidden), BF),
    )(counts[0, 0], token_acts[0, 0])
    all_acts = lax.all_gather(acts, "edp", axis=0)
    all_grads = lax.all_to_all(
        out_grad[0, 0].reshape(groups, rows, columns), "edp", split_axis=0, concat_axis=0, tiled=True
    )
    grads = call(
        grad_kernel,
        1,
        (n,),
        [
            pl.BlockSpec((groups, piece, columns), lambda i, me: (0, me[0] ^ i, 0)),
            whole(groups, slots, tok, hidden),
        ],
        [whole(slots, piece, hidden)] * n,
        [jax.ShapeDtypeStruct((slots, piece, hidden), BF)] * n,
        [pltpu.VMEM((groups * slots * tok, slots * hidden), BF)],
    )(me, all_grads, all_acts)
    grads = [grads[0]] + [swap(grads[k], k, n) for k in range(1, n)]

    chunks = piece // CHUNK
    mine = pl.BlockSpec((CHUNK, hidden), lambda i, me, *_: (me[0] * chunks + i, 0))
    part = lambda count: pl.BlockSpec((count, CHUNK, hidden), lambda i, *_: (0, i, 0))
    placed = call(
        functools.partial(update_kernel, n),
        4,
        (chunks,),
        [mine] * 3 + [part(3)] * (n - 1) + [part(slots)] * n,
        [part(3)] * n,
        [jax.ShapeDtypeStruct((3, piece, hidden), BF)] * n,
        [
            pltpu.VMEM((n, CHUNK, hidden), F32),
            pltpu.VMEM((n, 3, CHUNK, hidden), BF),
            pltpu.SMEM((n,), jnp.int32),
            pltpu.SMEM((n,), jnp.int32),
        ],
    )(me, old_expert, replica_of, new_expert, params, first, second, *state, *grads)

    final = [placed[0]] + [swap(placed[k], k, n) for k in range(1, n)]
    out = pl.BlockSpec((piece, hidden), lambda i, me: (me[0] ^ i, 0))
    step, first, second = call(
        unpack_kernel,
        1,
        (n,),
        [whole(3, piece, hidden)] * n,
        [out] * 3,
        [jax.ShapeDtypeStruct((rows, hidden), d) for d in (F32, BF, BF)],
    )(me, *final)
    return step[None], first[None], second[None]


def plain_local(
    token_acts, out_grad, counts, params, first_moment, second_moment, old_expert, replica_of, new_expert
):
    groups = lax.axis_size("edp")
    owners = lax.axis_size("ep")
    model_width = out_grad.shape[2]
    slots, tok, hidden = token_acts.shape[2:]
    rows = model_width // groups
    piece = rows * hidden // owners
    exchange = functools.partial(lax.all_to_all, axis_name="ep", split_axis=0, concat_axis=0, tiled=True)
    row = jnp.arange(tok, dtype=jnp.int32)
    live = row[None, :] < counts[0, 0][:, None]
    acts = jnp.where(live[:, :, None], token_acts[0, 0], jnp.zeros_like(token_acts[0, 0]))
    all_acts = lax.all_gather(acts, "edp", axis=0)
    all_grads = lax.all_to_all(
        out_grad[0, 0].reshape(groups, rows, slots * tok), "edp", split_axis=0, concat_axis=0, tiled=True
    ).reshape(groups, rows, slots, tok)
    slot_grads = jnp.einsum("adst,astf->sdf", all_grads, all_acts, preferred_element_type=F32)
    pieces = lambda array: exchange(array.astype(BF).reshape(owners, piece))
    own, replica = pieces(slot_grads[0]), pieces(slot_grads[1])
    sum_matrix = (replica_of[None, :] == old_expert[:, None]).astype(BF)
    move_matrix = (old_expert[None, :] == new_expert[:, None]).astype(BF)
    total = own.astype(F32) + jnp.dot(sum_matrix, replica, preferred_element_type=F32)
    updated = adam_update(
        pieces(params[0]).astype(F32), pieces(first_moment[0]), pieces(second_moment[0]), total
    )
    result = []
    for array, kind in zip(updated, (F32, BF, BF)):
        placed = jnp.dot(move_matrix, array.astype(BF), preferred_element_type=F32)
        result.append(exchange(placed.astype(BF)).astype(kind).reshape(1, rows, hidden))
    return tuple(result)


def local(token_acts, out_grad, *others):
    groups, n = lax.axis_size("edp"), lax.axis_size("ep")
    rows = out_grad.shape[2] // groups
    fast = n & (n - 1) == 0 and rows % (n * CHUNK) == 0
    return (fast_local if fast else plain_local)(token_acts, out_grad, *others)


def solution(mesh):
    return jax.shard_map(
        local,
        mesh=mesh,
        in_specs=(
            P("edp", "ep", None, None, None),
            P("edp", "ep", None, None),
            P("edp", "ep", None),
            P("ep", "edp", None),
            P("ep", "edp", None),
            P("ep", "edp", None),
            P(),
            P(),
            P(),
        ),
        out_specs=(P("ep", "edp", None), P("ep", "edp", None), P("ep", "edp", None)),
        check_vma=False,
    )
```

```python
import functools

import jax
import jax.numpy as jnp
from jax import lax
from jax.experimental import pallas as pl
from jax.experimental.pallas import tpu as pltpu
from jax.sharding import PartitionSpec as P

beta_one = 0.9
beta_two = 0.95
bias_one = 0.9999734386011124
bias_two = 0.994079470779666
decay_rate = 0.1
adam_eps = 1e-08

BF = jnp.bfloat16
F32 = jnp.float32
CHUNK = 16
PARTS = 2
LIMIT = 56 * 1024 * 1024


def adam_update(weights, first_old, second_old, gradient):
    first_new = beta_one * first_old.astype(F32) + (1.0 - beta_one) * gradient
    second_new = beta_two * second_old.astype(F32) + (1.0 - beta_two) * gradient * gradient
    scaled = first_new / bias_one / (jnp.sqrt(second_new / bias_two) + adam_eps)
    step_new = -(scaled + decay_rate * weights)
    return step_new, first_new, second_new


def spread_kernel(me, counts, grads, acts, *outs):
    at = pl.program_id(0)
    slots, tok, hidden = acts.shape
    rows, columns = grads.shape
    row = lax.broadcasted_iota(jnp.int32, (tok, 1), 0)
    for j, out in enumerate(outs):

        @pl.when(at == j)
        def _(out=out):
            out[:rows] = grads[...]
            for s in range(slots):
                live = jnp.where(row < counts[s], acts[s], jnp.zeros_like(acts[s]))
                for b in range(hidden // columns):
                    to = rows + b * columns + s * tok
                    out[to : to + tok] = live[:, b * columns : (b + 1) * columns]


def pack_kernel(me, params, first, second, *outs):
    at = pl.program_id(0)
    for j, out in enumerate(outs):

        @pl.when(at == j)
        def _(out=out):
            out[0] = params[...].astype(BF)
            out[1] = first[...]
            out[2] = second[...]


def grad_kernel(rows, slots, tok, hidden, me, *refs):
    at = pl.program_id(0)
    groups = lax.axis_size("edp")
    given, outs, table = refs[:groups], refs[groups:-1], refs[-1]
    n = lax.axis_size("ep")
    parts = len(outs) // n
    columns = given[0].shape[1]
    piece = outs[0].shape[1]
    width = hidden // parts

    @pl.when(at == 0)
    def _():
        table[...] = jnp.zeros_like(table)
        for g in range(groups):
            for s in range(slots):
                for b in range(hidden // columns):
                    source = rows + b * columns + s * tok
                    table[
                        g * columns + s * tok : g * columns + (s + 1) * tok,
                        s * hidden + b * columns : s * hidden + (b + 1) * columns,
                    ] = given[g][source : source + tok]

    here = pl.ds(pl.multiple_of((me[0] ^ at) * piece, CHUNK), piece)
    left = jnp.concatenate([given[g][here] for g in range(groups)], axis=1)
    total = jnp.dot(left, table[...], preferred_element_type=F32).astype(BF)
    for j in range(n):

        @pl.when(at == j)
        def _(j=j):
            for p in range(parts):
                for s in range(slots):
                    start = s * hidden + p * width
                    outs[p * n + j][s] = total[:, start : start + width]


def update_kernel(n, me_ref, old, rep, new, *refs):
    params, first, second = refs[:3]
    state = refs[3 : 3 + n - 1]
    grads = refs[2 + n : 2 + 2 * n]
    outs = refs[2 + 2 * n : 2 + 3 * n]
    sums, placed, owner, target = refs[2 + 3 * n :]
    me = me_ref[0]
    for e in range(n):
        owner[old[e]] = e
        target[new[e]] = e
    for k in range(n):
        sums[k] = grads[k][0].astype(F32)
    for k in range(n):
        at = me ^ owner[rep[me ^ k]]
        sums[at] = sums[at] + grads[k][1].astype(F32)
    for k in range(n):
        if k == 0:
            old_state = (params[...], first[...], second[...])
        else:
            old_state = (state[k - 1][0].astype(F32), state[k - 1][1], state[k - 1][2])
        step_new, first_new, second_new = adam_update(*old_state, sums[k])
        to = me ^ target[old[me ^ k]]
        placed[to, 0] = step_new.astype(BF)
        placed[to, 1] = first_new.astype(BF)
        placed[to, 2] = second_new.astype(BF)
    for k in range(n):
        outs[k][...] = placed[k]


def unpack_kernel(n, me, *refs):
    pieces, (step, first, second) = refs[:n], refs[-3:]
    at = pl.program_id(0)
    for j, piece in enumerate(pieces):

        @pl.when(at == j)
        def _(piece=piece):
            step[...] = piece[0].astype(F32)
            first[...] = piece[1]
            second[...] = piece[2]


def call(kernel, prefetch, grid, in_specs, out_specs, out_shape, scratch=(), aliases={}):
    return pl.pallas_call(
        kernel,
        grid_spec=pltpu.PrefetchScalarGridSpec(
            num_scalar_prefetch=prefetch,
            grid=grid,
            in_specs=in_specs,
            out_specs=out_specs,
            scratch_shapes=scratch,
        ),
        out_shape=out_shape,
        input_output_aliases=aliases,
        compiler_params=pltpu.CompilerParams(vmem_limit_bytes=LIMIT),
    )


def swap(array, k, axis):
    return lax.ppermute(array, axis, [(i, i ^ k) for i in range(lax.axis_size(axis))])


def fast_local(
    token_acts, out_grad, counts, params, first_moment, second_moment, old_expert, replica_of, new_expert
):
    groups = lax.axis_size("edp")
    n = lax.axis_size("ep")
    model_width, columns = out_grad.shape[2:]
    slots, tok, hidden = token_acts.shape[2:]
    rows = model_width // groups
    piece = rows // n
    width = hidden // PARTS
    me = lax.axis_index("ep").astype(jnp.int32).reshape(1)
    group = lax.axis_index("edp").astype(jnp.int32).reshape(1)
    params, first, second = params[0], first_moment[0], second_moment[0]
    whole = lambda *shape: pl.BlockSpec(shape, lambda i, *_: (0,) * len(shape))
    others = range(1, n)

    packed = {}
    for ks in ([k for k in reversed(others) if k % 2 == 0], [k for k in reversed(others) if k % 2]):

        def by_k(i, me, ks=ks):
            k = ks[-1]
            for j in range(len(ks) - 1):
                k = jnp.where(i == j, ks[j], k)
            return (me[0] ^ k, 0)

        made = call(
            pack_kernel,
            1,
            (len(ks),),
            [pl.BlockSpec((piece, hidden), by_k)] * 3,
            [whole(3, piece, hidden)] * len(ks),
            [jax.ShapeDtypeStruct((3, piece, hidden), BF)] * len(ks),
        )(me, params, first, second)
        packed.update(zip(ks, made))
    state = {k: swap(array, k, "ep") for k, array in packed.items()}

    tall = rows + slots * tok * (hidden // columns)
    spread = call(
        spread_kernel,
        2,
        (groups,),
        [pl.BlockSpec((rows, columns), lambda i, me, *_: (me[0] ^ i, 0)), whole(slots, tok, hidden)],
        [whole(tall, columns)] * groups,
        [jax.ShapeDtypeStruct((tall, columns), BF)] * groups,
    )(group, counts[0, 0], out_grad[0, 0], token_acts[0, 0])
    spread = [spread[0]] + [swap(spread[k], k, "edp") for k in range(1, groups)]
    made = call(
        functools.partial(grad_kernel, rows, slots, tok, hidden),
        1,
        (n,),
        [whole(tall, columns)] * groups,
        [whole(slots, piece, width)] * (n * PARTS),
        [jax.ShapeDtypeStruct((slots, piece, width), BF)] * (n * PARTS),
        [pltpu.VMEM((groups * columns, slots * hidden), BF)],
    )(me, *spread)
    grads = [
        [made[p * n]] + [swap(made[p * n + k], k, "ep") for k in others] for p in range(PARTS)
    ]

    result = [None] * 3
    chunks = piece // CHUNK
    for p in range(PARTS):
        mine = pl.BlockSpec((CHUNK, width), lambda i, me, *_: (me[0] * chunks + i, p))
        part = lambda count, at: pl.BlockSpec((count, CHUNK, width), lambda i, *_: (0, i, at))
        placed = call(
            functools.partial(update_kernel, n),
            4,
            (chunks,),
            [mine] * 3 + [part(3, p)] * (n - 1) + [part(slots, 0)] * n,
            [part(3, 0)] * n,
            [jax.ShapeDtypeStruct((3, piece, width), BF)] * n,
            [
                pltpu.VMEM((n, CHUNK, width), F32),
                pltpu.VMEM((n, 3, CHUNK, width), BF),
                pltpu.SMEM((n,), jnp.int32),
                pltpu.SMEM((n,), jnp.int32),
            ],
        )(
            me, old_expert, replica_of, new_expert, params, first, second,
            *[state[k] for k in others], *grads[p],
        )

        final = [placed[0]] + [swap(placed[k], k, "ep") for k in others]
        out = pl.BlockSpec((piece, width), lambda i, me: (me[0] ^ i, p))
        earlier = [] if p == 0 else result
        result = call(
            functools.partial(unpack_kernel, n),
            1,
            (n,),
            [whole(3, piece, width)] * n + [pl.BlockSpec(memory_space=pl.ANY)] * len(earlier),
            [out] * 3,
            [jax.ShapeDtypeStruct((rows, hidden), d) for d in (F32, BF, BF)],
            aliases={1 + n + j: j for j in range(len(earlier))},
        )(me, *final, *earlier)
    step, first, second = result
    return step[None], first[None], second[None]


def plain_local(
    token_acts, out_grad, counts, params, first_moment, second_moment, old_expert, replica_of, new_expert
):
    groups = lax.axis_size("edp")
    owners = lax.axis_size("ep")
    model_width = out_grad.shape[2]
    slots, tok, hidden = token_acts.shape[2:]
    rows = model_width // groups
    piece = rows * hidden // owners
    exchange = functools.partial(lax.all_to_all, axis_name="ep", split_axis=0, concat_axis=0, tiled=True)
    row = jnp.arange(tok, dtype=jnp.int32)
    live = row[None, :] < counts[0, 0][:, None]
    acts = jnp.where(live[:, :, None], token_acts[0, 0], jnp.zeros_like(token_acts[0, 0]))
    all_acts = lax.all_gather(acts, "edp", axis=0)
    all_grads = lax.all_to_all(
        out_grad[0, 0].reshape(groups, rows, slots * tok), "edp", split_axis=0, concat_axis=0, tiled=True
    ).reshape(groups, rows, slots, tok)
    slot_grads = jnp.einsum("adst,astf->sdf", all_grads, all_acts, preferred_element_type=F32)
    pieces = lambda array: exchange(array.astype(BF).reshape(owners, piece))
    own, replica = pieces(slot_grads[0]), pieces(slot_grads[1])
    sum_matrix = (replica_of[None, :] == old_expert[:, None]).astype(BF)
    move_matrix = (old_expert[None, :] == new_expert[:, None]).astype(BF)
    total = own.astype(F32) + jnp.dot(sum_matrix, replica, preferred_element_type=F32)
    updated = adam_update(
        pieces(params[0]).astype(F32), pieces(first_moment[0]), pieces(second_moment[0]), total
    )
    result = []
    for array, kind in zip(updated, (F32, BF, BF)):
        placed = jnp.dot(move_matrix, array.astype(BF), preferred_element_type=F32)
        result.append(exchange(placed.astype(BF)).astype(kind).reshape(1, rows, hidden))
    return tuple(result)


def local(token_acts, out_grad, *others):
    groups, n = lax.axis_size("edp"), lax.axis_size("ep")
    rows, columns = out_grad.shape[2] // groups, out_grad.shape[3]
    fast = groups & (groups - 1) == 0 and n & (n - 1) == 0 and rows % (n * CHUNK) == 0
    fast = fast and columns == 128 and token_acts.shape[4] % (128 * PARTS) == 0
    return (fast_local if fast else plain_local)(token_acts, out_grad, *others)


def solution(mesh):
    return jax.shard_map(
        local,
        mesh=mesh,
        in_specs=(
            P("edp", "ep", None, None, None),
            P("edp", "ep", None, None),
            P("edp", "ep", None),
            P("ep", "edp", None),
            P("ep", "edp", None),
            P("ep", "edp", None),
            P(),
            P(),
            P(),
        ),
        out_specs=(P("ep", "edp", None), P("ep", "edp", None), P("ep", "edp", None)),
        check_vma=False,
    )
```

```python
import functools

import jax
import jax.numpy as jnp
from jax import lax
from jax.experimental import pallas as pl
from jax.experimental.pallas import tpu as pltpu
from jax.sharding import PartitionSpec as P

beta_one = 0.9
beta_two = 0.95
bias_one = 0.9999734386011124
bias_two = 0.994079470779666
decay_rate = 0.1
adam_eps = 1e-08

BF = jnp.bfloat16
F32 = jnp.float32
CHUNK = 16
PARTS = 2
LIMIT = 56 * 1024 * 1024


def adam_update(weights, first_old, second_old, gradient):
    first_new = beta_one * first_old.astype(F32) + (1.0 - beta_one) * gradient
    second_new = beta_two * second_old.astype(F32) + (1.0 - beta_two) * gradient * gradient
    scaled = first_new / bias_one / (jnp.sqrt(second_new / bias_two) + adam_eps)
    step_new = -(scaled + decay_rate * weights)
    return step_new, first_new, second_new


def spread_kernel(me, counts, grads, acts, *outs):
    at = pl.program_id(0)
    slots, tok, hidden = acts.shape
    rows, columns = grads.shape
    row = lax.broadcasted_iota(jnp.int32, (tok, 1), 0)
    for j, out in enumerate(outs):

        @pl.when(at == j)
        def _(out=out):
            out[:rows] = grads[...]
            for s in range(slots):
                live = jnp.where(row < counts[s], acts[s], jnp.zeros_like(acts[s]))
                for b in range(hidden // columns):
                    to = rows + b * columns + s * tok
                    out[to : to + tok] = live[:, b * columns : (b + 1) * columns]


def pack_kernel(me, *refs):
    at = pl.program_id(0)
    params, first, second, *outs = refs
    for j, out in enumerate(outs):

        @pl.when(at == j)
        def _(out=out):
            out[0] = params[...].astype(BF)
            out[1] = first[...]
            out[2] = second[...]


def grad_kernel(rows, slots, tok, width, half, begin, me, *refs):
    at = pl.program_id(0)
    groups = lax.axis_size("edp")
    given, outs, table = refs[:groups], refs[groups:-1], refs[-1]
    columns = given[0].shape[1]
    piece = rows // 4
    core = me[0] & 1

    @pl.when(at == 0)
    def _():
        table[...] = jnp.zeros_like(table)
        for g in range(groups):
            for s in range(slots):
                for c in range(2):
                    for b in range(width // columns):
                        source = rows + c * half + begin + b * columns + s * tok
                        table[
                            c,
                            g * columns + s * tok : g * columns + (s + 1) * tok,
                            s * width + b * columns : s * width + (b + 1) * columns,
                        ] = given[g][source : source + tok]

    for i, (h, f) in enumerate(((0, 0), (1, 0), (0, 1), (1, 1))):

        @pl.when(at == i)
        def _(h=h, f=f):
            block = h * 2 + (side(me[0], h) ^ 1 ^ f)
            here = pl.ds(pl.multiple_of(block * piece, CHUNK), piece)
            left = jnp.concatenate([given[g][here] for g in range(groups)], axis=1)
            for c in range(2):
                total = jnp.dot(left, table[core ^ c], preferred_element_type=F32).astype(BF)
                for s in range(slots):
                    block = total[:, s * width : (s + 1) * width]
                    if c == 0:
                        outs[2 * f + h][s] = block
                    elif f == 0:
                        outs[4 + h][s] = block
                    else:
                        outs[6][h, s] = block


def side(me, h):
    return (me >> (1 + h)) & 1


def across(difference, h):
    return (difference >> (2 - h)) & 1


def member(difference, h):
    return (difference & 1) | (((difference >> (1 + h)) & 1) << 1)


def members(h):
    return (0, 1, 2 << h, (2 << h) | 1)


def find(n, names, places):
    for e in range(n):
        places[names[e]] = e


def cross_kernel(n, me_ref, old, rep, *refs):
    reps, outs, (sums, owner) = refs[:8], refs[8:10], refs[10:]
    me = me_ref[0]
    find(n, old, owner)
    for h in range(2):
        sums[...] = jnp.zeros_like(sums)
        for j, k in enumerate(members(h)):
            difference = owner[rep[me ^ k]] ^ me
            at = jnp.where(across(difference, h) == 1, member(difference, h), 4)
            sums[at] = sums[at] + reps[4 * h + j][0].astype(F32)
        outs[h][...] = sums[:4].astype(BF)


def update_kernel(n, crossing, me_ref, old, rep, new, *refs):
    mine, state, grads, partial = refs[:6], refs[6:12], refs[12:20], refs[20:22]
    stays, crosses = refs[22:24], refs[24 : 24 + 2 * (crossing > 0)]
    sums, placed, owner, target = refs[-4:]
    me = me_ref[0]
    find(n, old, owner)
    find(n, new, target)
    for h in range(2):
        for j in range(4):
            sums[j] = grads[4 * h + j][0].astype(F32) + partial[h][j].astype(F32)
        for j, k in enumerate(members(h)):
            difference = owner[rep[me ^ k]] ^ me
            at = jnp.where(across(difference, h) == 1, 4, member(difference, h))
            sums[at] = sums[at] + grads[4 * h + j][1].astype(F32)
        count = jnp.int32(4)
        for j, k in enumerate(members(h)):
            if j == 0:
                old_state = (mine[3 * h][...], mine[3 * h + 1][...], mine[3 * h + 2][...])
            else:
                ref = state[3 * h + j - 1]
                old_state = (ref[0].astype(F32), ref[1], ref[2])
            step_new, first_new, second_new = adam_update(*old_state, sums[j])
            difference = target[old[me ^ k]] ^ me
            moves = across(difference, h)
            to = jnp.where(moves == 1, count, member(difference, h))
            count = count + moves
            placed[to, 0] = step_new.astype(BF)
            placed[to, 1] = first_new.astype(BF)
            placed[to, 2] = second_new.astype(BF)
        stays[h][...] = placed[:4]
        if crossing:
            crosses[h][...] = placed[4 : 4 + crossing]


def merge_kernel(n, crossing, me_ref, old, new, *refs):
    stays, crossed = refs[:2], refs[2:4]
    kept, sibling, sent = refs[4:6], refs[6], refs[7:9]
    target, source = refs[9:]
    me = me_ref[0]
    find(n, new, target)
    for h in range(2):
        for j in range(4):
            source[j] = -1
        other = me ^ (4 >> h)
        count = jnp.int32(0)
        for k in members(h):
            owner = target[old[other ^ k]]
            moves = across(owner ^ other, h)
            place = jnp.where(moves == 1, member(owner ^ me, h), 4)
            source[place] = count
            count = count + moves
        for j in range(4):
            out = (kept[h], sibling.at[h], sent[h].at[0], sent[h].at[1])[j]

            @pl.when(source[j] < 0)
            def _(out=out, h=h, j=j):
                out[...] = stays[h][j]

            @pl.when(source[j] >= 0)
            def _(out=out, h=h, j=j):
                out[...] = crossed[h][source[j]]


def unpack_kernel(me, *refs):
    kept, sibling, came, passed = refs[:2], refs[2], refs[3:5], refs[5:7]
    step, first, second = refs[-3:]
    at = pl.program_id(0)
    for i in range(8):

        @pl.when(at == i)
        def _(h=i % 2, c=i // 2 % 2, f=i // 4):
            if f == 0:
                piece = kept[h] if c == 0 else sibling.at[h]
            else:
                piece = came[h].at[0] if c == 0 else passed[h].at[1]
            step[...] = piece[0].astype(F32)
            first[...] = piece[1]
            second[...] = piece[2]


def call(kernel, prefetch, grid, in_specs, out_specs, out_shape, scratch=(), aliases={}):
    return pl.pallas_call(
        kernel,
        grid_spec=pltpu.PrefetchScalarGridSpec(
            num_scalar_prefetch=prefetch,
            grid=grid,
            in_specs=in_specs,
            out_specs=out_specs,
            scratch_shapes=scratch,
        ),
        out_shape=out_shape,
        input_output_aliases=aliases,
        compiler_params=pltpu.CompilerParams(vmem_limit_bytes=LIMIT),
    )


def swap(array, k, axis):
    return lax.ppermute(array, axis, [(i, i ^ k) for i in range(lax.axis_size(axis))])


def fast_local(
    token_acts, out_grad, counts, params, first_moment, second_moment, old_expert, replica_of, new_expert
):
    groups = lax.axis_size("edp")
    n = lax.axis_size("ep")
    model_width, columns = out_grad.shape[2:]
    slots, tok, hidden = token_acts.shape[2:]
    rows = model_width // groups
    piece = rows // 4
    half = hidden // 2
    width = half // PARTS
    chunk = 2 * CHUNK if piece % (2 * CHUNK) == 0 else CHUNK
    me = lax.axis_index("ep").astype(jnp.int32).reshape(1)
    group = lax.axis_index("edp").astype(jnp.int32).reshape(1)
    params, first, second = params[0], first_moment[0], second_moment[0]
    whole = lambda *shape: pl.BlockSpec(shape, lambda i, *_: (0,) * len(shape))
    shape = lambda *dims: jax.ShapeDtypeStruct(dims, BF)
    sibling = lambda array: swap(array, 1, "ep")
    along = lambda array, h: swap(array, 2 << h, "ep")
    over = lambda array, h: swap(array, 4 >> h, "ep")

    def pack(keeps, c):
        def block(i, me):
            h = i % 2
            return (h * 2 + (((me[0] >> (1 + h)) & 1) ^ 1 ^ (i // 2)), (me[0] & 1) ^ c)

        return call(
            pack_kernel,
            1,
            (2 * keeps,),
            [pl.BlockSpec((piece, half), block)] * 3,
            [whole(3, piece, half)] * (2 * keeps),
            [shape(3, piece, half)] * (2 * keeps),
        )(me, params, first, second)

    state = [[None] * 3 for _ in range(2)]
    direct = pack(1, 0)
    for h in range(2):
        state[h][1] = along(direct[h], h)
    direct = pack(2, 1)
    for h in range(2):
        state[h][2] = along(sibling(direct[h]), h)
        state[h][0] = sibling(direct[2 + h])

    tall = rows + slots * tok * (hidden // columns)
    spread = call(
        spread_kernel,
        2,
        (groups,),
        [pl.BlockSpec((rows, columns), lambda i, me, *_: (me[0] ^ i, 0)), whole(slots, tok, hidden)],
        [whole(tall, columns)] * groups,
        [shape(tall, columns)] * groups,
    )(group, counts[0, 0], out_grad[0, 0], token_acts[0, 0])
    spread = [spread[0]] + [swap(spread[k], k, "edp") for k in range(1, groups)]
    grads, partial = [], []
    for p in range(PARTS):
        made = call(
            functools.partial(grad_kernel, rows, slots, tok, width, half, p * width),
            1,
            (4,),
            [whole(tall, columns)] * groups,
            [whole(slots, piece, width)] * 6 + [whole(2, slots, piece, width)],
            [shape(slots, piece, width)] * 6 + [shape(2, slots, piece, width)],
            [pltpu.VMEM((2, groups * columns, slots * width), BF)],
        )(me, *spread)
        near = sibling(made[6])
        grads.append(
            [[made[2 + h], near, along(made[h], h), along(sibling(made[4 + h]), h)] for h in range(2)]
        )

    def specs(slot):
        one = pl.BlockSpec((slots if slot is None else 1, chunk, width), lambda i, *_: (slot or 0, i, 0))
        two = lambda h: pl.BlockSpec(
            (None, slots if slot is None else 1, chunk, width), lambda i, *_: (h, slot or 0, i, 0)
        )
        return [one, two(0), one, one, one, two(1), one, one]

    four = lambda count: pl.BlockSpec((count, chunk, width), lambda i, *_: (0, i, 0))
    for p in range(PARTS):
        sums = call(
            functools.partial(cross_kernel, n),
            3,
            (piece // chunk,),
            specs(1),
            [four(4)] * 2,
            [shape(4, piece, width)] * 2,
            [pltpu.VMEM((5, chunk, width), F32), pltpu.SMEM((n,), jnp.int32)],
        )(me, old_expert, replica_of, *grads[p][0], *grads[p][1])
        partial.append([over(sums[h], h) for h in range(2)])

    def rest(crossing, params, first, second, state, grads, partial):
        placed = []
        for p in range(PARTS):

            def mine(h):
                return pl.BlockSpec(
                    (chunk, width),
                    lambda i, me, *_: (
                        (h * 2 + ((me[0] >> (1 + h)) & 1)) * (piece // chunk) + i,
                        (me[0] & 1) * PARTS + p,
                    ),
                )

            item = lambda count: pl.BlockSpec((count, 3, chunk, width), lambda i, *_: (0, 0, i, 0))
            held = pl.BlockSpec((3, chunk, width), lambda i, *_: (0, i, p))
            kinds = [4, 4] + [crossing] * (2 * (crossing > 0))
            made = call(
                functools.partial(update_kernel, n, crossing),
                4,
                (piece // chunk,),
                [mine(0)] * 3 + [mine(1)] * 3 + [held] * 6 + specs(None) + [four(4)] * 2,
                [item(count) for count in kinds],
                [shape(count, 3, piece, width) for count in kinds],
                [
                    pltpu.VMEM((5, chunk, width), F32),
                    pltpu.VMEM((8, 3, chunk, width), BF),
                    pltpu.SMEM((n,), jnp.int32),
                    pltpu.SMEM((n,), jnp.int32),
                ],
            )(
                me, old_expert, replica_of, new_expert, params, first, second, params, first, second,
                *state[0], *state[1], *grads[p][0], *grads[p][1], *partial[p],
            )
            crossed = [over(made[2 + h], h) for h in range(2)] if crossing else made[:2]
            placed.append((made[:2], crossed))

        result = []
        for p in range(PARTS):
            stays, crossed = placed[p]
            item = lambda *counts: pl.BlockSpec(
                (*counts, 3, chunk, width), lambda i, *_: (0,) * (len(counts) + 1) + (i, 0)
            )
            kinds = [(), (), (2,), (2,), (2,)]
            made = call(
                functools.partial(merge_kernel, n, crossing),
                3,
                (piece // chunk,),
                [item(4)] * 2 + [item(max(crossing, 1))] * 2,
                [item(*counts) for counts in kinds],
                [shape(*counts, 3, piece, width) for counts in kinds],
                [pltpu.SMEM((n,), jnp.int32), pltpu.SMEM((5,), jnp.int32)],
            )(me, old_expert, new_expert, *stays, *crossed)
            came = [along(made[3 + h], h) for h in range(2)]
            final = [made[0], made[1], sibling(made[2]), *came, *[sibling(array) for array in came]]

            def out(i, me, p=p):
                h, c, f = i % 2, i // 2 % 2, i // 4
                return (h * 2 + (((me[0] >> (1 + h)) & 1) ^ f), ((me[0] & 1) ^ c) * PARTS + p)

            result = call(
                unpack_kernel,
                1,
                (8,),
                [whole(3, piece, width)] * 2
                + [whole(2, 3, piece, width)] * 5
                + [pl.BlockSpec(memory_space=pl.ANY)] * len(result),
                [pl.BlockSpec((piece, width), out)] * 3,
                [jax.ShapeDtypeStruct((rows, hidden), d) for d in (F32, BF, BF)],
                aliases={8 + j: j for j in range(len(result))},
            )(me, *final, *result)
        return result

    index = jnp.arange(n, dtype=jnp.int32)
    difference = index[:, None] ^ index[None, :]
    both = across(difference, 0) + (across(difference, 1) << 16)
    both = jnp.sum(jnp.where(old_expert[:, None] == new_expert[None, :], both, 0))
    most = jnp.maximum(both >> 16, both & 0xFFFF) // 2
    step, first, second = lax.switch(
        most,
        [functools.partial(rest, crossing) for crossing in range(5)],
        params, first, second, state, grads, partial,
    )
    return step[None], first[None], second[None]


def plain_local(
    token_acts, out_grad, counts, params, first_moment, second_moment, old_expert, replica_of, new_expert
):
    groups = lax.axis_size("edp")
    owners = lax.axis_size("ep")
    model_width = out_grad.shape[2]
    slots, tok, hidden = token_acts.shape[2:]
    rows = model_width // groups
    piece = rows * hidden // owners
    exchange = functools.partial(lax.all_to_all, axis_name="ep", split_axis=0, concat_axis=0, tiled=True)
    row = jnp.arange(tok, dtype=jnp.int32)
    live = row[None, :] < counts[0, 0][:, None]
    acts = jnp.where(live[:, :, None], token_acts[0, 0], jnp.zeros_like(token_acts[0, 0]))
    all_acts = lax.all_gather(acts, "edp", axis=0)
    all_grads = lax.all_to_all(
        out_grad[0, 0].reshape(groups, rows, slots * tok), "edp", split_axis=0, concat_axis=0, tiled=True
    ).reshape(groups, rows, slots, tok)
    slot_grads = jnp.einsum("adst,astf->sdf", all_grads, all_acts, preferred_element_type=F32)
    pieces = lambda array: exchange(array.astype(BF).reshape(owners, piece))
    own, replica = pieces(slot_grads[0]), pieces(slot_grads[1])
    sum_matrix = (replica_of[None, :] == old_expert[:, None]).astype(BF)
    move_matrix = (old_expert[None, :] == new_expert[:, None]).astype(BF)
    total = own.astype(F32) + jnp.dot(sum_matrix, replica, preferred_element_type=F32)
    updated = adam_update(
        pieces(params[0]).astype(F32), pieces(first_moment[0]), pieces(second_moment[0]), total
    )
    result = []
    for array, kind in zip(updated, (F32, BF, BF)):
        placed = jnp.dot(move_matrix, array.astype(BF), preferred_element_type=F32)
        result.append(exchange(placed.astype(BF)).astype(kind).reshape(1, rows, hidden))
    return tuple(result)


def local(token_acts, out_grad, *others):
    groups, n = lax.axis_size("edp"), lax.axis_size("ep")
    rows, columns = out_grad.shape[2] // groups, out_grad.shape[3]
    slots, _, hidden = token_acts.shape[2:]
    fast = n == 8 and groups & (groups - 1) == 0 and rows % (4 * CHUNK) == 0
    fast = fast and slots == 2 and columns == 128 and hidden % (256 * PARTS) == 0
    return (fast_local if fast else plain_local)(token_acts, out_grad, *others)


def solution(mesh):
    return jax.shard_map(
        local,
        mesh=mesh,
        in_specs=(
            P("edp", "ep", None, None, None),
            P("edp", "ep", None, None),
            P("edp", "ep", None),
            P("ep", "edp", None),
            P("ep", "edp", None),
            P("ep", "edp", None),
            P(),
            P(),
            P(),
        ),
        out_specs=(P("ep", "edp", None), P("ep", "edp", None), P("ep", "edp", None)),
        check_vma=False,
    )
```

```python
import functools

import jax
import jax.numpy as jnp
from jax import lax
from jax.experimental import pallas as pl
from jax.experimental.pallas import tpu as pltpu
from jax.sharding import PartitionSpec as P

beta_one = 0.9
beta_two = 0.95
bias_one = 0.9999734386011124
bias_two = 0.994079470779666
decay_rate = 0.1
adam_eps = 1e-08

BF = jnp.bfloat16
F32 = jnp.float32
CHUNK = 16
PARTS = 2
LIMIT = 56 * 1024 * 1024


def adam_update(weights, first_old, second_old, gradient):
    first_new = beta_one * first_old.astype(F32) + (1.0 - beta_one) * gradient
    second_new = beta_two * second_old.astype(F32) + (1.0 - beta_two) * gradient * gradient
    scaled = first_new / bias_one / (jnp.sqrt(second_new / bias_two) + adam_eps)
    step_new = -(scaled + decay_rate * weights)
    return step_new, first_new, second_new


def quick_update(weights, first_old, second_old, gradient):
    first_new = beta_one * first_old.astype(F32) + (1.0 - beta_one) * gradient
    second_new = beta_two * second_old.astype(F32) + (1.0 - beta_two) * gradient * gradient
    unbiased = second_new * (1.0 / bias_two)
    root = unbiased * lax.rsqrt(unbiased) + adam_eps
    scaled = first_new * (-1.0 / bias_one) * pl.reciprocal(root, approx=True)
    return scaled - decay_rate * weights, first_new, second_new


def spread_kernel(slot, me, counts, grads, acts, *outs):
    at = pl.program_id(0)
    _, tok, hidden = acts.shape
    rows, columns = grads.shape
    row = lax.broadcasted_iota(jnp.int32, (tok, 1), 0)
    lane = lax.broadcasted_iota(jnp.int32, (1, columns), 1)
    for j, out in enumerate(outs):

        @pl.when(at == j)
        def _(out=out):
            top, bottom = grads[: rows // 2].astype(F32), grads[rows // 2 :].astype(F32)
            if slot == 0:
                bottom = pltpu.roll(bottom, tok, 1)
            else:
                top = pltpu.roll(top, tok, 1)
            out[: rows // 2] = jnp.where(lane < tok, top, bottom).astype(BF)
            live = jnp.where(row < counts[slot], acts[0], jnp.zeros_like(acts[0]))
            for b in range(hidden // columns):
                to = rows // 2 + b * tok
                out[to : to + tok] = live[:, b * columns : (b + 1) * columns]


def pack_kernel(me, *refs):
    at = pl.program_id(0)
    params, first, second, *outs = refs
    for j, out in enumerate(outs):

        @pl.when(at == j)
        def _(out=out):
            out[0] = params[...].astype(BF)
            out[1] = first[...]
            out[2] = second[...]


def grad_kernel(rows, tok, me, *refs):
    at = pl.program_id(0)
    groups = lax.axis_size("edp")
    given, outs, table = refs[:groups], refs[groups:-1], refs[-1]
    columns = given[0].shape[1]
    piece, half = outs[0].shape
    core = me[0] & 1

    @pl.when(at == 0)
    def _():
        for g in range(groups):
            for c in range(2):
                for b in range(half // columns):
                    source = rows // 2 + (c * half // columns + b) * tok
                    block = given[g][source : source + tok]
                    for h in range(2):
                        to = g * columns + h * tok
                        table[c, to : to + tok, b * columns : (b + 1) * columns] = block

    lane = lax.broadcasted_iota(jnp.int32, (1, groups * columns), 1) % columns
    for i, (h, f) in enumerate(((0, 0), (1, 0), (0, 1), (1, 1))):

        @pl.when(at == i)
        def _(h=h, f=f):
            here = pl.ds(pl.multiple_of((side(me[0], h) ^ 1 ^ f) * piece, CHUNK), piece)
            left = jnp.concatenate([given[g][here] for g in range(groups)], axis=1)
            left = jnp.where(lane // tok == h, left, jnp.zeros_like(left))
            for c in range(2):
                total = jnp.dot(left, table[core ^ c], preferred_element_type=F32).astype(BF)
                if c == 0:
                    outs[2 * f + h][...] = total
                elif f == 0:
                    outs[4 + h][...] = total
                else:
                    outs[6][h] = total


def side(me, h):
    return (me >> (1 + h)) & 1


def across(difference, h):
    return (difference >> (2 - h)) & 1


def member(difference, h):
    return (difference & 1) | (((difference >> (1 + h)) & 1) << 1)


def members(h):
    return (0, 1, 2 << h, (2 << h) | 1)


def find(n, names, places):
    for e in range(n):
        places[names[e]] = e


def cross_kernel(n, me_ref, old, rep, *refs):
    reps, outs, (sums, owner) = refs[:8], refs[8:12], refs[12:]
    me = me_ref[0]
    find(n, old, owner)
    for h in range(2):
        sums[...] = jnp.zeros_like(sums)
        for j, k in enumerate(members(h)):
            difference = owner[rep[me ^ k]] ^ me
            at = member(difference, h) + 4 * across(difference, h)
            sums[at] = sums[at] + reps[4 * h + j][...].astype(F32)
        outs[h][...] = sums[4:].astype(BF)
        outs[2 + h][...] = sums[:4].astype(BF)


def update_kernel(n, crossing, me_ref, old, new, *refs):
    mine, state, grads, here, there = refs[:6], refs[6:12], refs[12:20], refs[20:22], refs[22:24]
    stays, crosses = refs[24:26], refs[26 : 26 + 2 * (crossing > 0)]
    target = refs[-1]
    me = me_ref[0]
    find(n, new, target)
    for h in range(2):
        count = jnp.int32(0)
        for j, k in enumerate(members(h)):
            gradient = grads[4 * h + j][...].astype(F32) + here[h][j].astype(F32) + there[h][j].astype(F32)
            if j == 0:
                old_state = (mine[3 * h][...], mine[3 * h + 1][...], mine[3 * h + 2][...])
            else:
                ref = state[3 * h + j - 1]
                old_state = (ref[0].astype(F32), ref[1], ref[2])
            updated = [array.astype(BF) for array in quick_update(*old_state, gradient)]
            difference = target[old[me ^ k]] ^ me
            moves = across(difference, h)

            @pl.when(moves == 0)
            def _(h=h, to=member(difference, h), updated=updated):
                for i in range(3):
                    stays[h][to, i] = updated[i]

            if crossing:

                @pl.when(moves == 1)
                def _(h=h, to=count, updated=updated):
                    for i in range(3):
                        crosses[h][to, i] = updated[i]

            count = count + moves


def merge_kernel(n, crossing, me_ref, old, new, *refs):
    stays, crossed = refs[:2], refs[2:4]
    kept, sibling, sent = refs[4], refs[5], refs[6:8]
    target, source, sems = refs[8:]
    me = me_ref[0]
    find(n, new, target)
    for h in range(2):
        for j in range(4):
            source[5 * h + j] = -1
        other = me ^ (4 >> h)
        count = jnp.int32(0)
        for k in members(h):
            owner = target[old[other ^ k]]
            moves = across(owner ^ other, h)
            place = jnp.where(moves == 1, member(owner ^ me, h), 4)
            source[5 * h + place] = count
            count = count + moves

    def each(act):
        for h in range(2):
            for j in range(4):
                out = (kept.at[h], sibling.at[h], sent[h].at[0], sent[h].at[1])[j]
                where = source[5 * h + j]
                sem = sems.at[4 * h + j]

                @pl.when(where < 0)
                def _(out=out, h=h, j=j, sem=sem):
                    act(pltpu.make_async_copy(stays[h].at[j], out, sem))

                if crossing:

                    @pl.when(where >= 0)
                    def _(out=out, h=h, where=where, sem=sem):
                        act(pltpu.make_async_copy(crossed[h].at[where], out, sem))

    each(lambda copy: copy.start())
    each(lambda copy: copy.wait())


def unpack_kernel(part, f, me_ref, *refs):
    pieces, (step, first, second), (given, wide, came, went) = refs[:4], refs[-7:-4], refs[-4:]
    me = me_ref[0]
    _, piece, width = given.shape

    def place(i):
        h, c = i // 2, i % 2
        row = pl.multiple_of((h * 2 + (side(me, h) ^ f)) * piece, CHUNK)
        column = pl.multiple_of((((me & 1) ^ c) * PARTS + part) * width, 128)
        return pl.ds(row, piece), pl.ds(column, width)

    arrive, leave = [], []
    for i in range(4):
        h, c = i // 2, i % 2
        ref = pieces[c].at[h] if f == 0 else pieces[2 * c + h].at[c]
        arrive.append(pltpu.make_async_copy(ref.at[0], given.at[i], came.at[i]))
        leave.append(pltpu.make_async_copy(ref.at[1], first.at[place(i)], went.at[3 * i]))
        leave.append(pltpu.make_async_copy(ref.at[2], second.at[place(i)], went.at[3 * i + 1]))
    for copy in arrive + leave:
        copy.start()
    for i in range(4):
        arrive[i].wait()
        wide[i] = given[i].astype(F32)
        leave.append(pltpu.make_async_copy(wide.at[i], step.at[place(i)], went.at[3 * i + 2]))
        leave[-1].start()
    for copy in leave:
        copy.wait()


def call(kernel, prefetch, grid, in_specs, out_specs, out_shape, scratch=(), aliases={}):
    return pl.pallas_call(
        kernel,
        grid_spec=pltpu.PrefetchScalarGridSpec(
            num_scalar_prefetch=prefetch,
            grid=grid,
            in_specs=in_specs,
            out_specs=out_specs,
            scratch_shapes=scratch,
        ),
        out_shape=out_shape,
        input_output_aliases=aliases,
        compiler_params=pltpu.CompilerParams(vmem_limit_bytes=LIMIT),
    )


def swap(array, k, axis):
    return lax.ppermute(array, axis, [(i, i ^ k) for i in range(lax.axis_size(axis))])


def fast_local(
    token_acts, out_grad, counts, params, first_moment, second_moment, old_expert, replica_of, new_expert
):
    groups = lax.axis_size("edp")
    n = lax.axis_size("ep")
    model_width, columns = out_grad.shape[2:]
    slots, tok, hidden = token_acts.shape[2:]
    rows = model_width // groups
    piece = rows // 4
    half = hidden // 2
    width = half // PARTS
    chunk = 2 * CHUNK if piece % (2 * CHUNK) == 0 else CHUNK
    me = lax.axis_index("ep").astype(jnp.int32).reshape(1)
    group = lax.axis_index("edp").astype(jnp.int32).reshape(1)
    params, first, second = params[0], first_moment[0], second_moment[0]
    whole = lambda *shape: pl.BlockSpec(shape, lambda i, *_: (0,) * len(shape))
    shape = lambda *dims: jax.ShapeDtypeStruct(dims, BF)
    sibling = lambda array: swap(array, 1, "ep")
    along = lambda array, h: swap(array, 2 << h, "ep")
    over = lambda array, h: swap(array, 4 >> h, "ep")

    def pack(keeps, c):
        def block(i, me):
            h = i % 2
            return (h * 2 + (((me[0] >> (1 + h)) & 1) ^ 1 ^ (i // 2)), (me[0] & 1) ^ c)

        return call(
            pack_kernel,
            1,
            (2 * keeps,),
            [pl.BlockSpec((piece, half), block)] * 3,
            [whole(3, piece, half)] * (2 * keeps),
            [shape(3, piece, half)] * (2 * keeps),
        )(me, params, first, second)

    state = [[None] * 3 for _ in range(2)]
    direct = pack(1, 0)
    for h in range(2):
        state[h][1] = along(direct[h], h)
    direct = pack(2, 1)
    for h in range(2):
        state[h][2] = along(sibling(direct[h]), h)
        state[h][0] = sibling(direct[2 + h])

    tall = rows // 2 + tok * (hidden // columns)

    def slot_grads(slot):
        spread = call(
            functools.partial(spread_kernel, slot),
            2,
            (groups,),
            [
                pl.BlockSpec((rows, columns), lambda i, me, *_: (me[0] ^ i, 0)),
                pl.BlockSpec((1, tok, hidden), lambda i, *_: (slot, 0, 0)),
            ],
            [whole(tall, columns)] * groups,
            [shape(tall, columns)] * groups,
        )(group, counts[0, 0], out_grad[0, 0], token_acts[0, 0])
        spread = [spread[0]] + [swap(spread[k], k, "edp") for k in range(1, groups)]
        made = call(
            functools.partial(grad_kernel, rows, tok),
            1,
            (4,),
            [whole(tall, columns)] * groups,
            [whole(piece, half)] * 6 + [whole(2, piece, half)],
            [shape(piece, half)] * 6 + [shape(2, piece, half)],
            [pltpu.VMEM((2, groups * columns, half), BF)],
        )(me, *spread)
        near = sibling(made[6])
        grads = []
        for h in range(2):
            grads += [made[2 + h], near, along(made[h], h), along(sibling(made[4 + h]), h)]
        return grads

    def specs(wide, at):
        one = pl.BlockSpec((chunk, wide), lambda i, *_: (i, at))
        two = lambda h: pl.BlockSpec((None, chunk, wide), lambda i, *_: (h, i, at))
        return [one, two(0), one, one, one, two(1), one, one]

    replica = slot_grads(1)
    four = lambda wide, at: pl.BlockSpec((4, chunk, wide), lambda i, *_: (0, i, at))
    sums = call(
        functools.partial(cross_kernel, n),
        3,
        (piece // chunk,),
        specs(half, 0),
        [four(half, 0)] * 4,
        [shape(4, piece, half)] * 4,
        [pltpu.VMEM((8, chunk, half), F32), pltpu.SMEM((n,), jnp.int32)],
    )(me, old_expert, replica_of, *replica)
    there = [over(sums[h], h) for h in range(2)]
    here = sums[2:]
    own = slot_grads(0)

    def rest(crossing, params, first, second, state, own, here, there):
        placed = []
        for p in range(PARTS):

            def mine(h):
                return pl.BlockSpec(
                    (chunk, width),
                    lambda i, me, *_: (
                        (h * 2 + ((me[0] >> (1 + h)) & 1)) * (piece // chunk) + i,
                        (me[0] & 1) * PARTS + p,
                    ),
                )

            item = lambda count: pl.BlockSpec((count, 3, chunk, width), lambda i, *_: (0, 0, i, 0))
            held = pl.BlockSpec((3, chunk, width), lambda i, *_: (0, i, p))
            kinds = [4, 4] + [crossing] * (2 * (crossing > 0))
            made = call(
                functools.partial(update_kernel, n, crossing),
                3,
                (piece // chunk,),
                [mine(0)] * 3 + [mine(1)] * 3 + [held] * 6 + specs(width, p) + [four(width, p)] * 4,
                [item(count) for count in kinds],
                [shape(count, 3, piece, width) for count in kinds],
                [pltpu.SMEM((n,), jnp.int32)],
            )(
                me, old_expert, new_expert, params, first, second, params, first, second,
                *state[0], *state[1], *own, *here, *there,
            )
            crossed = [over(made[2 + h], h) for h in range(2)] if crossing else made[:2]
            placed.append((made[:2], crossed))

        any_ = pl.BlockSpec(memory_space=pl.ANY)
        result = []
        for p in range(PARTS):
            stays, crossed = placed[p]
            made = call(
                functools.partial(merge_kernel, n, crossing),
                3,
                (),
                [any_] * 4,
                [any_] * 4,
                [shape(2, 3, piece, width)] * 4,
                [
                    pltpu.SMEM((n,), jnp.int32),
                    pltpu.SMEM((10,), jnp.int32),
                    pltpu.SemaphoreType.DMA((8,)),
                ],
            )(me, old_expert, new_expert, *stays, *crossed)
            came = [along(made[2 + h], h) for h in range(2)]
            passed = [sibling(array) for array in came]
            for f, pieces in enumerate(([made[0], sibling(made[1])], came + passed)):
                result = call(
                    functools.partial(unpack_kernel, p, f),
                    1,
                    (),
                    [any_] * (len(pieces) + len(result)),
                    [pl.BlockSpec(memory_space=pltpu.HBM)] * 3,
                    [jax.ShapeDtypeStruct((rows, hidden), d) for d in (F32, BF, BF)],
                    [
                        pltpu.VMEM((4, piece, width), BF),
                        pltpu.VMEM((4, piece, width), F32),
                        pltpu.SemaphoreType.DMA((4,)),
                        pltpu.SemaphoreType.DMA((12,)),
                    ],
                    {1 + len(pieces) + j: j for j in range(len(result))},
                )(me, *pieces, *result)
        return result

    index = jnp.arange(n, dtype=jnp.int32)
    difference = index[:, None] ^ index[None, :]
    both = across(difference, 0) + (across(difference, 1) << 16)
    both = jnp.sum(jnp.where(old_expert[:, None] == new_expert[None, :], both, 0))
    most = jnp.maximum(both >> 16, both & 0xFFFF) // 2
    step, first, second = lax.switch(
        most,
        [functools.partial(rest, crossing) for crossing in range(5)],
        params, first, second, state, own, here, there,
    )
    return step[None], first[None], second[None]


def plain_local(
    token_acts, out_grad, counts, params, first_moment, second_moment, old_expert, replica_of, new_expert
):
    groups = lax.axis_size("edp")
    owners = lax.axis_size("ep")
    model_width = out_grad.shape[2]
    slots, tok, hidden = token_acts.shape[2:]
    rows = model_width // groups
    piece = rows * hidden // owners
    exchange = functools.partial(lax.all_to_all, axis_name="ep", split_axis=0, concat_axis=0, tiled=True)
    row = jnp.arange(tok, dtype=jnp.int32)
    live = row[None, :] < counts[0, 0][:, None]
    acts = jnp.where(live[:, :, None], token_acts[0, 0], jnp.zeros_like(token_acts[0, 0]))
    all_acts = lax.all_gather(acts, "edp", axis=0)
    all_grads = lax.all_to_all(
        out_grad[0, 0].reshape(groups, rows, slots * tok), "edp", split_axis=0, concat_axis=0, tiled=True
    ).reshape(groups, rows, slots, tok)
    slot_grads = jnp.einsum("adst,astf->sdf", all_grads, all_acts, preferred_element_type=F32)
    pieces = lambda array: exchange(array.astype(BF).reshape(owners, piece))
    own, replica = pieces(slot_grads[0]), pieces(slot_grads[1])
    sum_matrix = (replica_of[None, :] == old_expert[:, None]).astype(BF)
    move_matrix = (old_expert[None, :] == new_expert[:, None]).astype(BF)
    total = own.astype(F32) + jnp.dot(sum_matrix, replica, preferred_element_type=F32)
    updated = adam_update(
        pieces(params[0]).astype(F32), pieces(first_moment[0]), pieces(second_moment[0]), total
    )
    result = []
    for array, kind in zip(updated, (F32, BF, BF)):
        placed = jnp.dot(move_matrix, array.astype(BF), preferred_element_type=F32)
        result.append(exchange(placed.astype(BF)).astype(kind).reshape(1, rows, hidden))
    return tuple(result)


def local(token_acts, out_grad, *others):
    groups, n = lax.axis_size("edp"), lax.axis_size("ep")
    rows, columns = out_grad.shape[2] // groups, out_grad.shape[3]
    slots, tok, hidden = token_acts.shape[2:]
    fast = n == 8 and groups & (groups - 1) == 0 and rows % (4 * CHUNK) == 0
    fast = fast and slots == 2 and columns == 128 and tok == 64 and hidden % (256 * PARTS) == 0
    return (fast_local if fast else plain_local)(token_acts, out_grad, *others)


def solution(mesh):
    return jax.shard_map(
        local,
        mesh=mesh,
        in_specs=(
            P("edp", "ep", None, None, None),
            P("edp", "ep", None, None),
            P("edp", "ep", None),
            P("ep", "edp", None),
            P("ep", "edp", None),
            P("ep", "edp", None),
            P(),
            P(),
            P(),
        ),
        out_specs=(P("ep", "edp", None), P("ep", "edp", None), P("ep", "edp", None)),
        check_vma=False,
    )
```

```python
import functools

import jax
import jax.numpy as jnp
from jax import lax
from jax.experimental import pallas as pl
from jax.experimental.pallas import tpu as pltpu
from jax.sharding import PartitionSpec as P

beta_one = 0.9
beta_two = 0.95
bias_one = 0.9999734386011124
bias_two = 0.994079470779666
decay_rate = 0.1
adam_eps = 1e-08

BF = jnp.bfloat16
F32 = jnp.float32
CHUNK = 16
PARTS = 2
LIMIT = 56 * 1024 * 1024


def adam_update(weights, first_old, second_old, gradient):
    first_new = beta_one * first_old.astype(F32) + (1.0 - beta_one) * gradient
    second_new = beta_two * second_old.astype(F32) + (1.0 - beta_two) * gradient * gradient
    scaled = first_new / bias_one / (jnp.sqrt(second_new / bias_two) + adam_eps)
    step_new = -(scaled + decay_rate * weights)
    return step_new, first_new, second_new


def quick_update(weights, first_old, second_old, gradient):
    first_new = beta_one * first_old.astype(F32) + (1.0 - beta_one) * gradient
    second_new = beta_two * second_old.astype(F32) + (1.0 - beta_two) * gradient * gradient
    unbiased = second_new * (1.0 / bias_two)
    root = unbiased * lax.rsqrt(unbiased) + adam_eps
    scaled = first_new * (-1.0 / bias_one) * pl.reciprocal(root, approx=True)
    return scaled - decay_rate * weights, first_new, second_new


def spread_kernel(slot, groups, me, counts, grads, acts, *refs):
    at = pl.program_id(0)
    outs = refs[-groups:]
    _, tok, hidden = acts.shape
    rows, columns = grads.shape
    row = lax.broadcasted_iota(jnp.int32, (tok, 1), 0)
    lane = lax.broadcasted_iota(jnp.int32, (1, columns), 1)
    for j, out in enumerate(outs):

        @pl.when(at == j)
        def _(out=out):
            top, bottom = grads[: rows // 2].astype(F32), grads[rows // 2 :].astype(F32)
            if slot == 0:
                bottom = pltpu.roll(bottom, tok, 1)
            else:
                top = pltpu.roll(top, tok, 1)
            out[: rows // 2] = jnp.where(lane < tok, top, bottom).astype(BF)
            live = jnp.where(row < counts[slot], acts[0], jnp.zeros_like(acts[0]))
            for b in range(hidden // columns):
                to = rows // 2 + b * tok
                out[to : to + tok] = live[:, b * columns : (b + 1) * columns]


def pack_kernel(me, params, first, second, *outs):
    at = pl.program_id(0)
    for j, out in enumerate(outs):
        for i in range(2):

            @pl.when(at == 2 * j + i)
            def _(out=out, i=i):
                out[i, 0] = params[...].astype(BF)
                out[i, 1] = first[...]
                out[i, 2] = second[...]


def grad_kernel(rows, tok, me, *refs):
    at = pl.program_id(0)
    groups = lax.axis_size("edp")
    given, outs, table = refs[:groups], refs[groups:-1], refs[-1]
    columns = given[0].shape[1]
    _, piece, half = outs[0].shape
    core = me[0] & 1

    @pl.when(at == 0)
    def _():
        for g in range(groups):
            for c in range(2):
                for b in range(half // columns):
                    source = rows // 2 + (c * half // columns + b) * tok
                    block = given[g][source : source + tok]
                    for h in range(2):
                        to = g * columns + h * tok
                        table[c, to : to + tok, b * columns : (b + 1) * columns] = block

    lane = lax.broadcasted_iota(jnp.int32, (1, groups * columns), 1) % columns
    for i, (h, f) in enumerate(((0, 0), (1, 0), (0, 1), (1, 1))):

        @pl.when(at == i)
        def _(h=h, f=f):
            here = pl.ds(pl.multiple_of((side(me[0], h) ^ 1 ^ f) * piece, CHUNK), piece)
            left = jnp.concatenate([given[g][here] for g in range(groups)], axis=1)
            left = jnp.where(lane // tok == h, left, jnp.zeros_like(left))
            for c in range(2):
                total = jnp.dot(left, table[core ^ c], preferred_element_type=F32).astype(BF)
                if f == 0:
                    outs[h][c] = total
                else:
                    outs[2 + c][h] = total


def side(me, h):
    return (me >> (1 + h)) & 1


def across(difference, h):
    return (difference >> (2 - h)) & 1


def member(difference, h):
    return (difference & 1) | (((difference >> (1 + h)) & 1) << 1)


def members(h):
    return (0, 1, 2 << h, (2 << h) | 1)


def find(n, names, places):
    for e in range(n):
        places[names[e]] = e


def cross_kernel(n, me_ref, old, rep, *refs):
    reps, outs, owner = refs[:8], refs[8:12], refs[12]
    me = me_ref[0]
    find(n, old, owner)
    for h in range(2):
        places = []
        for k in members(h):
            difference = owner[rep[me ^ k]] ^ me
            places.append(member(difference, h) + 4 * across(difference, h))
        weights = [[jnp.where(place == j, 1.0, 0.0) for place in places] for j in range(8)]

        def add(r, _, h=h, weights=weights):
            rows = pl.ds(pl.multiple_of(r * CHUNK, CHUNK), CHUNK)
            parts = [reps[4 * h + j][rows].astype(F32) for j in range(4)]
            for j in range(8):
                total = weights[j][0] * parts[0]
                for weight, part in zip(weights[j][1:], parts[1:]):
                    total = total + weight * part
                outs[h if j >= 4 else 2 + h][j % 4, rows] = total.astype(BF)
            return 0

        lax.fori_loop(0, reps[0].shape[0] // CHUNK, add, 0)


def update_kernel(n, crossing, me_ref, old, new, *refs):
    mine, state, grads, here, there = refs[:6], refs[6:12], refs[12:20], refs[20:22], refs[22:24]
    home, sent, crosses = refs[24:26], refs[26:28], refs[28 : 28 + 2 * (crossing > 0)]
    target = refs[-1]
    me = me_ref[0]
    find(n, new, target)
    for h in range(2):
        count = jnp.int32(0)
        for j, k in enumerate(members(h)):
            difference = target[old[me ^ k]] ^ me
            moves = across(difference, h)
            to = member(difference, h)

            def put(out, at, h=h, j=j):
                def update(r, _):
                    rows = pl.ds(pl.multiple_of(r * CHUNK, CHUNK), CHUNK)
                    gradient = grads[4 * h + j][rows].astype(F32) + here[h][j, rows].astype(F32)
                    gradient = gradient + there[h][j, rows].astype(F32)
                    if j == 0:
                        old_state = [mine[3 * h + i][rows] for i in range(3)]
                    else:
                        old_state = [state[3 * h + j - 1][i, rows] for i in range(3)]
                    for i, array in enumerate(quick_update(old_state[0].astype(F32), *old_state[1:], gradient)):
                        out[at, i, rows] = array.astype(BF)
                    return 0

                lax.fori_loop(0, mine[0].shape[0] // CHUNK, update, 0)

            @pl.when((moves == 0) & (to < 2))
            def _(h=h, put=put, to=to):
                put(home[h], to)

            @pl.when((moves == 0) & (to >= 2))
            def _(h=h, put=put, to=to):
                put(sent[h], to - 2)

            if crossing:

                @pl.when(moves == 1)
                def _(h=h, put=put, count=count):
                    put(crosses[h], count)

            count = count + moves


def merge_kernel(n, crossing, me_ref, old, new, *refs):
    crossed, home, sent = refs[:2], refs[6:8], refs[8:10]
    target, place, buffer, arrive, leave = refs[10:]
    me = me_ref[0]
    find(n, new, target)
    for h in range(2):
        other = me ^ (4 >> h)
        for i in range(4):
            place[4 * h + i] = -1
        count = jnp.int32(0)
        for k in members(h):
            owner = target[old[other ^ k]]
            moves = across(owner ^ other, h)

            @pl.when(moves == 1)
            def _(h=h, count=count, owner=owner):
                place[4 * h + count] = member(owner ^ me, h)

            count = count + moves
    slots = [(h, i) for h in range(2) for i in range(crossing)]

    def out(act, h, i):
        to, at = place[4 * h + i], crossing * h + i
        for j in range(4):

            @pl.when(to == j)
            def _(ref=(home[h], sent[h])[j // 2].at[j % 2]):
                act(pltpu.make_async_copy(buffer.at[at], ref, leave.at[at]))

    def into(h, i):
        at = crossing * h + i
        return pltpu.make_async_copy(crossed[h].at[i], buffer.at[at], arrive.at[at])

    for h, i in slots:
        into(h, i).start()
    for h, i in slots:
        into(h, i).wait()
        out(lambda copy: copy.start(), h, i)
    for h, i in slots:
        out(lambda copy: copy.wait(), h, i)


def unpack_kernel(part, f, me_ref, *refs):
    pieces, (step, first, second), (given, wide, came, went) = refs[:4], refs[-7:-4], refs[-4:]
    me = me_ref[0]
    piece, width = given.shape[2:]

    def place(i):
        h, c = i // 2, i % 2
        row = pl.multiple_of((h * 2 + (side(me, h) ^ f)) * piece, CHUNK)
        column = pl.multiple_of((((me & 1) ^ c) * PARTS + part) * width, 128)
        return pl.ds(row, piece), pl.ds(column, width)

    arrive, leave = [], []
    for i in range(4):
        h, c = i // 2, i % 2
        arrive.append(pltpu.make_async_copy(pieces[2 * c + h].at[c], given.at[i], came.at[i]))
        arrive[-1].start()
    for i in range(4):
        arrive[i].wait()
        leave.append(pltpu.make_async_copy(given.at[i, 1], first.at[place(i)], went.at[3 * i]))
        leave.append(pltpu.make_async_copy(given.at[i, 2], second.at[place(i)], went.at[3 * i + 1]))
        leave[-2].start()
        leave[-1].start()
        wide[i] = given[i, 0].astype(F32)
        leave.append(pltpu.make_async_copy(wide.at[i], step.at[place(i)], went.at[3 * i + 2]))
        leave[-1].start()
    for copy in leave:
        copy.wait()


def call(kernel, prefetch, grid, in_specs, out_specs, out_shape, scratch=(), aliases={}):
    return pl.pallas_call(
        kernel,
        grid_spec=pltpu.PrefetchScalarGridSpec(
            num_scalar_prefetch=prefetch,
            grid=grid,
            in_specs=in_specs,
            out_specs=out_specs,
            scratch_shapes=scratch,
        ),
        out_shape=out_shape,
        input_output_aliases=aliases,
        compiler_params=pltpu.CompilerParams(vmem_limit_bytes=LIMIT),
    )


def swap(array, k, axis):
    return lax.ppermute(array, axis, [(i, i ^ k) for i in range(lax.axis_size(axis))])


def fast_local(
    token_acts, out_grad, counts, params, first_moment, second_moment, old_expert, replica_of, new_expert
):
    groups = lax.axis_size("edp")
    n = lax.axis_size("ep")
    model_width, columns = out_grad.shape[2:]
    slots, tok, hidden = token_acts.shape[2:]
    rows = model_width // groups
    piece = rows // 4
    half = hidden // 2
    width = half // PARTS
    chunk = piece // 2 if piece % (2 * CHUNK) == 0 else CHUNK
    me = lax.axis_index("ep").astype(jnp.int32).reshape(1)
    group = lax.axis_index("edp").astype(jnp.int32).reshape(1)
    params, first, second = params[0], first_moment[0], second_moment[0]
    whole = lambda *shape: pl.BlockSpec(shape, lambda i, *_: (0,) * len(shape))
    shape = lambda *dims: jax.ShapeDtypeStruct(dims, BF)
    any_ = pl.BlockSpec(memory_space=pl.ANY)
    sibling = lambda array: swap(array, 1, "ep")
    along = lambda array, h: swap(array, 2 << h, "ep")
    over = lambda array, h: swap(array, 4 >> h, "ep")

    tall = rows // 2 + tok * (hidden // columns)

    def exchange(slot, after):
        spread = call(
            functools.partial(spread_kernel, slot, groups),
            2,
            (groups,),
            [
                pl.BlockSpec((rows, columns), lambda i, me, *_: (me[0] ^ i, 0)),
                pl.BlockSpec((1, tok, hidden), lambda i, *_: (slot, 0, 0)),
            ]
            + [any_] * len(after),
            [whole(tall, columns)] * groups,
            [shape(tall, columns)] * groups,
        )(group, counts[0, 0], out_grad[0, 0], token_acts[0, 0], *after)
        return [spread[0]] + [swap(spread[k], k, "edp") for k in range(1, groups)]

    def pack(blocks, count):
        return call(
            pack_kernel,
            1,
            (2 * count,),
            [pl.BlockSpec((piece, half), blocks)] * 3,
            [whole(2, 3, piece, half)] * count,
            [shape(2, 3, piece, half)] * count,
        )(me, params, first, second)

    def to_send(i, me):
        h = i // 2
        return (h * 2 + (((me[0] >> (1 + h)) & 1) ^ 1), (me[0] & 1) ^ (i % 2))

    def to_keep(i, me):
        return (i * 2 + ((me[0] >> (1 + i)) & 1), (me[0] & 1) ^ 1)

    replica = exchange(1, [])
    sends = pack(to_send, 2)
    state = [along(sends[h], h) for h in range(2)]
    own = exchange(0, [sends[0], *replica[1:]])
    (kept,) = pack(to_keep, 1)
    state = [sibling(kept), *state, *[sibling(array) for array in state]]

    def slot_grads(given):
        made = call(
            functools.partial(grad_kernel, rows, tok),
            1,
            (4,),
            [whole(tall, columns)] * groups,
            [whole(2, piece, half)] * 4,
            [shape(2, piece, half)] * 4,
            [pltpu.VMEM((2, groups * columns, half), BF)],
        )(me, *given)
        came = [along(made[h], h) for h in range(2)]
        return [made[2], sibling(made[3]), *came, *[sibling(array) for array in came]]

    def members_of(arrays):
        kept, near, *others = arrays
        return [
            part for h in range(2) for part in ((kept, h), (near, h), (others[h], 0), (others[2 + h], 1))
        ]

    def specs(members, *block, at=0):
        middle = (0,) * (len(block) - 2)
        return [
            pl.BlockSpec((None, *block), lambda i, *_, slot=slot: (slot, *middle, i, at)) for _, slot in members
        ]

    arrays = lambda members: [array for array, _ in members]
    replica = members_of(slot_grads(replica))
    four = lambda wide, at: pl.BlockSpec((4, chunk, wide), lambda i, *_: (0, i, at))
    sums = call(
        functools.partial(cross_kernel, n),
        3,
        (piece // chunk,),
        specs(replica, chunk, half),
        [four(half, 0)] * 4,
        [shape(4, piece, half)] * 4,
        [pltpu.SMEM((n,), jnp.int32)],
    )(me, old_expert, replica_of, *arrays(replica))
    there = [over(sums[h], h) for h in range(2)]
    here = sums[2:]
    own = slot_grads(own)

    def rest(crossing, params, first, second, state, own, here, there):
        own = members_of(own)
        near, *others = state
        state = [
            part for h in range(2) for part in ((near, h), (others[h], 0), (others[2 + h], 1))
        ]
        result = []
        for p in range(PARTS):

            def mine(h):
                return pl.BlockSpec(
                    (chunk, width),
                    lambda i, me, *_: (
                        (h * 2 + ((me[0] >> (1 + h)) & 1)) * (piece // chunk) + i,
                        (me[0] & 1) * PARTS + p,
                    ),
                )

            item = lambda count: pl.BlockSpec((count, 3, chunk, width), lambda i, *_: (0, 0, i, 0))
            kinds = [2] * 4 + [crossing] * (2 * (crossing > 0))
            made = call(
                functools.partial(update_kernel, n, crossing),
                3,
                (piece // chunk,),
                [mine(0)] * 3
                + [mine(1)] * 3
                + specs(state, 3, chunk, width, at=p)
                + specs(own, chunk, width, at=p)
                + [four(width, p)] * 4,
                [item(count) for count in kinds],
                [shape(count, 3, piece, width) for count in kinds],
                [pltpu.SMEM((n,), jnp.int32)],
            )(
                me, old_expert, new_expert, params, first, second, params, first, second,
                *arrays(state), *arrays(own), *here, *there,
            )
            crossed = [over(array, h) for h, array in enumerate(made[4:])]
            result.append((made[:4], crossed))
        if crossing:
            result = [
                call(
                    functools.partial(merge_kernel, n, crossing),
                    3,
                    (),
                    [any_] * 6,
                    [any_] * 4,
                    [shape(2, 3, piece, width)] * 4,
                    [
                        pltpu.SMEM((n,), jnp.int32),
                        pltpu.SMEM((8,), jnp.int32),
                        pltpu.VMEM((2 * crossing, 3, piece, width), BF),
                        pltpu.SemaphoreType.DMA((2 * crossing,)),
                        pltpu.SemaphoreType.DMA((2 * crossing,)),
                    ],
                    {5 + j: j for j in range(4)},
                )(me, old_expert, new_expert, *crossed, *made)
                for made, crossed in result
            ]
        else:
            result = [made for made, _ in result]
        return [list(made) for made in result]

    index = jnp.arange(n, dtype=jnp.int32)
    difference = index[:, None] ^ index[None, :]
    both = across(difference, 0) + (across(difference, 1) << 16)
    both = jnp.sum(jnp.where(old_expert[:, None] == new_expert[None, :], both, 0))
    most = jnp.maximum(both >> 16, both & 0xFFFF) // 2
    placed = lax.switch(
        most,
        [functools.partial(rest, crossing) for crossing in range(5)],
        params, first, second, state, own, here, there,
    )

    result = []
    for p in range(PARTS):
        home, sent = placed[p][:2], placed[p][2:]
        came = [along(sent[h], h) for h in range(2)]
        for f, pieces in enumerate((home, came)):
            pieces = [*pieces, *[sibling(array) for array in pieces]]
            result = call(
                functools.partial(unpack_kernel, p, f),
                1,
                (),
                [any_] * (4 + len(result)),
                [pl.BlockSpec(memory_space=pltpu.HBM)] * 3,
                [jax.ShapeDtypeStruct((rows, hidden), d) for d in (F32, BF, BF)],
                [
                    pltpu.VMEM((4, 3, piece, width), BF),
                    pltpu.VMEM((4, piece, width), F32),
                    pltpu.SemaphoreType.DMA((4,)),
                    pltpu.SemaphoreType.DMA((12,)),
                ],
                {5 + j: j for j in range(len(result))},
            )(me, *pieces, *result)
    step, first, second = result
    return step[None], first[None], second[None]


def plain_local(
    token_acts, out_grad, counts, params, first_moment, second_moment, old_expert, replica_of, new_expert
):
    groups = lax.axis_size("edp")
    owners = lax.axis_size("ep")
    model_width = out_grad.shape[2]
    slots, tok, hidden = token_acts.shape[2:]
    rows = model_width // groups
    piece = rows * hidden // owners
    exchange = functools.partial(lax.all_to_all, axis_name="ep", split_axis=0, concat_axis=0, tiled=True)
    row = jnp.arange(tok, dtype=jnp.int32)
    live = row[None, :] < counts[0, 0][:, None]
    acts = jnp.where(live[:, :, None], token_acts[0, 0], jnp.zeros_like(token_acts[0, 0]))
    all_acts = lax.all_gather(acts, "edp", axis=0)
    all_grads = lax.all_to_all(
        out_grad[0, 0].reshape(groups, rows, slots * tok), "edp", split_axis=0, concat_axis=0, tiled=True
    ).reshape(groups, rows, slots, tok)
    slot_grads = jnp.einsum("adst,astf->sdf", all_grads, all_acts, preferred_element_type=F32)
    pieces = lambda array: exchange(array.astype(BF).reshape(owners, piece))
    own, replica = pieces(slot_grads[0]), pieces(slot_grads[1])
    sum_matrix = (replica_of[None, :] == old_expert[:, None]).astype(BF)
    move_matrix = (old_expert[None, :] == new_expert[:, None]).astype(BF)
    total = own.astype(F32) + jnp.dot(sum_matrix, replica, preferred_element_type=F32)
    updated = adam_update(
        pieces(params[0]).astype(F32), pieces(first_moment[0]), pieces(second_moment[0]), total
    )
    result = []
    for array, kind in zip(updated, (F32, BF, BF)):
        placed = jnp.dot(move_matrix, array.astype(BF), preferred_element_type=F32)
        result.append(exchange(placed.astype(BF)).astype(kind).reshape(1, rows, hidden))
    return tuple(result)


def local(token_acts, out_grad, *others):
    groups, n = lax.axis_size("edp"), lax.axis_size("ep")
    rows, columns = out_grad.shape[2] // groups, out_grad.shape[3]
    slots, tok, hidden = token_acts.shape[2:]
    fast = n == 8 and groups & (groups - 1) == 0 and rows % (4 * CHUNK) == 0
    fast = fast and slots == 2 and columns == 128 and tok == 64 and hidden % (256 * PARTS) == 0
    return (fast_local if fast else plain_local)(token_acts, out_grad, *others)


def solution(mesh):
    return jax.shard_map(
        local,
        mesh=mesh,
        in_specs=(
            P("edp", "ep", None, None, None),
            P("edp", "ep", None, None),
            P("edp", "ep", None),
            P("ep", "edp", None),
            P("ep", "edp", None),
            P("ep", "edp", None),
            P(),
            P(),
            P(),
        ),
        out_specs=(P("ep", "edp", None), P("ep", "edp", None), P("ep", "edp", None)),
        check_vma=False,
    )
```

```python
import functools

import jax
import jax.numpy as jnp
from jax import lax
from jax.experimental import pallas as pl
from jax.experimental.pallas import tpu as pltpu
from jax.sharding import PartitionSpec as P

beta_one = 0.9
beta_two = 0.95
bias_one = 0.9999734386011124
bias_two = 0.994079470779666
decay_rate = 0.1
adam_eps = 1e-08

BF = jnp.bfloat16
F32 = jnp.float32
CHUNK = 16
PARTS = 2
LIMIT = 61 * 1024 * 1024


def adam_update(weights, first_old, second_old, gradient):
    first_new = beta_one * first_old.astype(F32) + (1.0 - beta_one) * gradient
    second_new = beta_two * second_old.astype(F32) + (1.0 - beta_two) * gradient * gradient
    scaled = first_new / bias_one / (jnp.sqrt(second_new / bias_two) + adam_eps)
    step_new = -(scaled + decay_rate * weights)
    return step_new, first_new, second_new


def quick_update(weights, first_old, second_old, gradient):
    first_new = beta_one * first_old.astype(F32) + (1.0 - beta_one) * gradient
    second_new = beta_two * second_old.astype(F32) + (1.0 - beta_two) * gradient * gradient
    unbiased = second_new * (1.0 / bias_two)
    root = unbiased * lax.rsqrt(unbiased) + adam_eps
    scaled = first_new * (-1.0 / bias_one) * pl.reciprocal(root, approx=True)
    return scaled - decay_rate * weights, first_new, second_new


def spread_kernel(group, counts, grads, acts, *refs):
    outs = refs[1:]
    slots, tok, hidden = acts.shape
    columns = grads.shape[1]
    rows = grads.shape[0] // len(outs)
    row = lax.broadcasted_iota(jnp.int32, (tok, 1), 0)
    live = [jnp.where(row < counts[s], acts[s], jnp.zeros_like(acts[s])) for s in range(slots)]
    for k, out in enumerate(outs):
        start = pl.multiple_of((group[0] ^ k) * rows, CHUNK)
        out[:rows] = grads[pl.ds(start, rows)]
        for s in range(slots):
            for b in range(hidden // columns):
                to = rows + b * slots * tok + s * tok
                out[to : to + tok] = live[s][:, b * columns : (b + 1) * columns]


def pack_kernel(items, me, params, first, second, *refs):
    at = pl.program_id(0)
    for i, (j, _) in enumerate(items):

        @pl.when(at == i)
        def _(out=refs[-2:][j]):
            out[0] = params[...].astype(BF)
            out[1] = first[...]
            out[2] = second[...]


def grad_kernel(rows, part, hidden, me, *refs):
    at = pl.program_id(0)
    groups = lax.axis_size("edp")
    given, outs, table = refs[:groups], refs[-6:-1], refs[-1]
    columns = given[0].shape[1]
    slots, _, piece, width = outs[0].shape
    tok = columns // slots
    core = me[0] & 1

    @pl.when(at == 0)
    def _():
        zero = jnp.zeros((tok, columns), BF)
        for g in range(groups):
            for c in range(2):
                for b in range(width // columns):
                    block = (c * (hidden // 2) + part * width) // columns + b
                    for t in range(slots):
                        source = rows + (block * slots + t) * tok
                        for s in range(slots):
                            to = g * columns + t * tok
                            at = s * width + b * columns
                            table[c, to : to + tok, at : at + columns] = (
                                given[g][source : source + tok] if s == t else zero
                            )

    chip = jnp.where(at == 3, 0, at + 1)
    here = pl.ds(pl.multiple_of(((me[0] >> 1) ^ chip) * piece, CHUNK), piece)
    left = jnp.concatenate([given[g][here] for g in range(groups)], axis=1)
    for c in range(2):
        total = jnp.dot(left, table[core ^ c], preferred_element_type=F32).astype(BF)
        for i in range(4):

            @pl.when(at == i)
            def _(i=i, c=c, total=total):
                for s in range(slots):
                    block = total[:, s * width : (s + 1) * width]
                    if i < 3:
                        outs[i][s, c] = block
                    else:
                        outs[3 + c][s] = block


def find(n, names, places):
    for e in range(n):
        places[names[e]] = e


def update_kernel(n, me_ref, old, rep, new, *refs):
    mine, state, grads, outs = refs[:3], refs[3 : 2 + n], refs[2 + n : 2 + 2 * n], refs[-8:-4]
    sums, placed, owner, target = refs[-4:]
    me = me_ref[0]
    find(n, old, owner)
    find(n, new, target)
    to = [target[old[me ^ k]] ^ me for k in range(n)]
    serves = [owner[rep[me ^ k]] ^ me for k in range(n)]

    def update(r, _):
        rows = pl.ds(pl.multiple_of(r * CHUNK, CHUNK), CHUNK)
        for k in range(n):
            sums[k] = grads[k][0, rows].astype(F32)
        for k in range(n):
            sums[serves[k]] = sums[serves[k]] + grads[k][1, rows].astype(F32)
        for k in range(n):
            old_state = [ref[rows] for ref in mine] if k == 0 else [state[k - 1][i, rows] for i in range(3)]
            updated = quick_update(old_state[0].astype(F32), *old_state[1:], sums[k])
            for i, array in enumerate(updated):
                placed[to[k], i] = array.astype(BF)
        for chip in range(4):
            outs[chip][:, :, rows] = placed[2 * chip : 2 * chip + 2]
        return 0

    lax.fori_loop(0, mine[0].shape[0] // CHUNK, update, 0)


def unpack_kernel(part, me_ref, *refs):
    (step, first, second), (given, wide, came, went) = refs[-7:-4], refs[-4:]
    me = me_ref[0]
    count, _, piece, width = given.shape
    pieces = refs[:count]

    def place(i):
        chip, c = i // 2, i % 2
        row = pl.multiple_of(((me >> 1) ^ chip) * piece, CHUNK)
        column = pl.multiple_of((((me & 1) ^ c) * PARTS + part) * width, 128)
        return pl.ds(row, piece), pl.ds(column, width)

    arrive, leave = [], []
    for i in range(count):
        arrive.append(pltpu.make_async_copy(pieces[i].at[i % 2], given.at[i], came.at[i]))
        arrive[-1].start()
    for i in range(count):
        arrive[i].wait()
        leave.append(pltpu.make_async_copy(given.at[i, 1], first.at[place(i)], went.at[3 * i]))
        leave.append(pltpu.make_async_copy(given.at[i, 2], second.at[place(i)], went.at[3 * i + 1]))
        leave[-2].start()
        leave[-1].start()
        wide[i] = given[i, 0].astype(F32)
        leave.append(pltpu.make_async_copy(wide.at[i], step.at[place(i)], went.at[3 * i + 2]))
        leave[-1].start()
    for copy in leave:
        copy.wait()


def order_kernel(*refs):
    pass


def call(kernel, prefetch, grid, in_specs, out_specs, out_shape, scratch=(), aliases={}):
    return pl.pallas_call(
        kernel,
        grid_spec=pltpu.PrefetchScalarGridSpec(
            num_scalar_prefetch=prefetch,
            grid=grid,
            in_specs=in_specs,
            out_specs=out_specs,
            scratch_shapes=scratch,
        ),
        out_shape=out_shape,
        input_output_aliases=aliases,
        compiler_params=pltpu.CompilerParams(vmem_limit_bytes=LIMIT),
    )


def swap(array, k, axis):
    return lax.ppermute(array, axis, [(i, i ^ k) for i in range(lax.axis_size(axis))])


def fast_local(
    token_acts, out_grad, counts, params, first_moment, second_moment, old_expert, replica_of, new_expert
):
    groups = lax.axis_size("edp")
    n = lax.axis_size("ep")
    model_width, columns = out_grad.shape[2:]
    slots, tok, hidden = token_acts.shape[2:]
    rows = model_width // groups
    piece = rows // 4
    half = hidden // 2
    width = half // PARTS
    chunk = piece // 2 if piece % (2 * CHUNK) == 0 else CHUNK
    me = lax.axis_index("ep").astype(jnp.int32).reshape(1)
    group = lax.axis_index("edp").astype(jnp.int32).reshape(1)
    params, first, second = params[0], first_moment[0], second_moment[0]
    whole = lambda *shape: pl.BlockSpec(shape, lambda i, *_: (0,) * len(shape))
    shape = lambda *dims: jax.ShapeDtypeStruct(dims, BF)
    hbm = pl.BlockSpec(memory_space=pltpu.HBM)
    sibling = lambda array: swap(array, 1, "ep")

    def order(after, *arrays):
        return call(
            order_kernel,
            0,
            (),
            [hbm] * (len(arrays) + len(after)),
            [hbm] * len(arrays),
            [jax.ShapeDtypeStruct(array.shape, array.dtype) for array in arrays],
            aliases={j: j for j in range(len(arrays))},
        )(*arrays, *after)

    def members(kept, near, came, passed):
        result = [(kept, None), (near, None)]
        for here, there in zip(came, passed):
            result += [(here, 0), (there, 1)]
        return result

    def pack(items, chips, shapes, after):
        def block(i, me):
            chip, c = chips[-1]
            for j in range(len(chips) - 1):
                chip = jnp.where(i == j, chips[j][0], chip)
                c = jnp.where(i == j, chips[j][1], c)
            return ((me[0] >> 1) ^ chip, (me[0] & 1) ^ c)

        def slot_spec(j):
            begin = min(i for i, (to, _) in enumerate(items) if to == j)
            last = shapes[j][0] - 1
            return pl.BlockSpec(
                (None, 3, piece, half), lambda i, *_: (jnp.clip(i - begin, 0, last), 0, 0, 0)
            )

        return call(
            functools.partial(pack_kernel, items),
            1,
            (len(items),),
            [pl.BlockSpec((piece, half), block)] * 3 + [hbm] * len(after),
            [slot_spec(j) for j in range(2)],
            [shape(*dims) for dims in shapes],
        )(me, params, first, second, *after)

    two, one = (2, 3, piece, half), (1, 3, piece, half)
    sends = pack([(0, 0), (0, 1), (1, 0), (1, 1)], [(1, 0), (1, 1), (2, 0), (2, 1)], [two, two], [])
    came = [swap(array, 2 + 2 * j, "ep") for j, array in enumerate(sends)]

    tall = rows + slots * tok * (hidden // columns)
    spread = call(
        spread_kernel,
        2,
        (1,),
        [whole(model_width, columns), whole(slots, tok, hidden), hbm],
        [whole(tall, columns)] * groups,
        [shape(tall, columns)] * groups,
    )(group, counts[0, 0], out_grad[0, 0], token_acts[0, 0], sends[0])
    given = [spread[0]] + [swap(spread[k], k, "edp") for k in range(1, groups)]

    diagonal, near = pack([(0, 0), (0, 1), (1, 0)], [(3, 0), (3, 1), (0, 1)], [two, one], [spread[0]])
    last = swap(diagonal, 6, "ep")

    def part_grads(p, after):
        sent, kept = (slots, 2, piece, width), (slots, piece, width)
        return call(
            functools.partial(grad_kernel, rows, p, hidden),
            1,
            (4,),
            [whole(tall, columns)] * groups + [hbm] * len(after),
            [whole(*sent)] * 3 + [whole(*kept)] * 2,
            [shape(*sent)] * 3 + [shape(*kept)] * 2,
            [pltpu.VMEM((2, groups * columns, slots * width), BF)],
        )(me, *given, *after)

    state = [(sibling(near), 0)]
    for array in came:
        state += [(array, 0), (sibling(array), 1)]
    made = [part_grads(0, [state[j][0] for j in (0, 2, 4)])]
    for p in range(1, PARTS):
        made.append(part_grads(p, [made[-1][3]]))
    done = [made[-1][3]]
    last, *others = order(done, last, *[parts[4] for parts in made])
    state += [(last, 0), (sibling(last), 1)]
    grads = []
    for p in range(PARTS):
        arrived = [swap(array, 2 + 2 * j, "ep") for j, array in enumerate(made[p][:3])]
        arrived = order(done, *arrived)
        grads.append([(made[p][3], None), (sibling(others[p]), None)])
        for array in arrived:
            grads[p] += [(array, 0), (sibling(array), 1)]

    def grad_spec(slot):
        if slot is None:
            return pl.BlockSpec((slots, chunk, width), lambda i, *_: (0, i, 0))
        return pl.BlockSpec((slots, None, chunk, width), lambda i, *_: (0, slot, i, 0))

    result = []
    for p in range(PARTS):
        mine = pl.BlockSpec(
            (chunk, width), lambda i, me, *_: ((me[0] >> 1) * (piece // chunk) + i, (me[0] & 1) * PARTS + p)
        )
        held = lambda slot: pl.BlockSpec((None, 3, chunk, width), lambda i, *_: (slot, 0, i, p))
        home, *sent = call(
            functools.partial(update_kernel, n),
            4,
            (piece // chunk,),
            [mine] * 3 + [held(slot) for _, slot in state] + [grad_spec(slot) for _, slot in grads[p]],
            [pl.BlockSpec((2, 3, chunk, width), lambda i, *_: (0, 0, i, 0))] * 4,
            [shape(2, 3, piece, width)] * 4,
            [
                pltpu.VMEM((n, CHUNK, width), F32),
                pltpu.VMEM((n, 3, CHUNK, width), BF),
                pltpu.SMEM((n,), jnp.int32),
                pltpu.SMEM((n,), jnp.int32),
            ],
        )(
            me, old_expert, replica_of, new_expert, params, first, second,
            *[array for array, _ in state], *[array for array, _ in grads[p]],
        )

        if p + 1 < PARTS:
            after = [grads[p + 1][j][0] for j in (3, 5)]
            sent[2:] = order(after, *sent[2:])
        else:
            sent[1:] = order([pieces[1], pieces[3]], *sent[1:])
        arrived = [swap(array, 2 + 2 * j, "ep") for j, array in enumerate(sent)]
        if result:
            arrived = order(result, *arrived)
        pieces = [part for array in [home, *arrived] for part in (array, sibling(array))]
        result = call(
            functools.partial(unpack_kernel, p),
            1,
            (),
            [hbm] * (len(pieces) + len(result)),
            [hbm] * 3,
            [jax.ShapeDtypeStruct((rows, hidden), d) for d in (F32, BF, BF)],
            [
                pltpu.VMEM((len(pieces), 3, piece, width), BF),
                pltpu.VMEM((len(pieces), piece, width), F32),
                pltpu.SemaphoreType.DMA((len(pieces),)),
                pltpu.SemaphoreType.DMA((3 * len(pieces),)),
            ],
            {1 + len(pieces) + j: j for j in range(len(result))},
        )(me, *pieces, *result)
    step, first, second = result
    return step[None], first[None], second[None]


def plain_local(
    token_acts, out_grad, counts, params, first_moment, second_moment, old_expert, replica_of, new_expert
):
    groups = lax.axis_size("edp")
    owners = lax.axis_size("ep")
    model_width = out_grad.shape[2]
    slots, tok, hidden = token_acts.shape[2:]
    rows = model_width // groups
    piece = rows * hidden // owners
    exchange = functools.partial(lax.all_to_all, axis_name="ep", split_axis=0, concat_axis=0, tiled=True)
    row = jnp.arange(tok, dtype=jnp.int32)
    live = row[None, :] < counts[0, 0][:, None]
    acts = jnp.where(live[:, :, None], token_acts[0, 0], jnp.zeros_like(token_acts[0, 0]))
    all_acts = lax.all_gather(acts, "edp", axis=0)
    all_grads = lax.all_to_all(
        out_grad[0, 0].reshape(groups, rows, slots * tok), "edp", split_axis=0, concat_axis=0, tiled=True
    ).reshape(groups, rows, slots, tok)
    slot_grads = jnp.einsum("adst,astf->sdf", all_grads, all_acts, preferred_element_type=F32)
    pieces = lambda array: exchange(array.astype(BF).reshape(owners, piece))
    own, replica = pieces(slot_grads[0]), pieces(slot_grads[1])
    sum_matrix = (replica_of[None, :] == old_expert[:, None]).astype(BF)
    move_matrix = (old_expert[None, :] == new_expert[:, None]).astype(BF)
    total = own.astype(F32) + jnp.dot(sum_matrix, replica, preferred_element_type=F32)
    updated = adam_update(
        pieces(params[0]).astype(F32), pieces(first_moment[0]), pieces(second_moment[0]), total
    )
    result = []
    for array, kind in zip(updated, (F32, BF, BF)):
        placed = jnp.dot(move_matrix, array.astype(BF), preferred_element_type=F32)
        result.append(exchange(placed.astype(BF)).astype(kind).reshape(1, rows, hidden))
    return tuple(result)


def local(token_acts, out_grad, *others):
    groups, n = lax.axis_size("edp"), lax.axis_size("ep")
    rows, columns = out_grad.shape[2] // groups, out_grad.shape[3]
    slots, tok, hidden = token_acts.shape[2:]
    fast = n == 8 and groups & (groups - 1) == 0 and rows % (4 * CHUNK) == 0
    fast = fast and slots == 2 and columns == 128 and tok == 64 and hidden % (256 * PARTS) == 0
    return (fast_local if fast else plain_local)(token_acts, out_grad, *others)


def solution(mesh):
    return jax.shard_map(
        local,
        mesh=mesh,
        in_specs=(
            P("edp", "ep", None, None, None),
            P("edp", "ep", None, None),
            P("edp", "ep", None),
            P("ep", "edp", None),
            P("ep", "edp", None),
            P("ep", "edp", None),
            P(),
            P(),
            P(),
        ),
        out_specs=(P("ep", "edp", None), P("ep", "edp", None), P("ep", "edp", None)),
        check_vma=False,
    )
```

```python
import functools

import jax
import jax.numpy as jnp
from jax import lax
from jax.experimental import pallas as pl
from jax.experimental.pallas import tpu as pltpu
from jax.sharding import PartitionSpec as P

beta_one = 0.9
beta_two = 0.95
bias_one = 0.9999734386011124
bias_two = 0.994079470779666
decay_rate = 0.1
adam_eps = 1e-08

BF = jnp.bfloat16
F32 = jnp.float32
CHUNK = 16
LIMIT = 56 * 1024 * 1024
FINE = 256
SPLIT = (2, 2)
ORDER = (0, 6, 2, 4, 3, 5, 7, 1)


def adam_update(weights, first_old, second_old, gradient):
    first_new = beta_one * first_old.astype(F32) + (1.0 - beta_one) * gradient
    second_new = beta_two * second_old.astype(F32) + (1.0 - beta_two) * gradient * gradient
    scaled = first_new / bias_one / (jnp.sqrt(second_new / bias_two) + adam_eps)
    step_new = -(scaled + decay_rate * weights)
    return step_new, first_new, second_new


def quick_update(weights, first_old, second_old, gradient):
    first_new = beta_one * first_old.astype(F32) + (1.0 - beta_one) * gradient
    second_new = beta_two * second_old.astype(F32) + (1.0 - beta_two) * gradient * gradient
    unbiased = second_new * (1.0 / bias_two)
    root = unbiased * lax.rsqrt(unbiased) + adam_eps
    scaled = first_new * (-1.0 / bias_one) * pl.reciprocal(root, approx=True)
    return scaled - decay_rate * weights, first_new, second_new


def spread_kernel(group, counts, grads, acts, *refs):
    outs = refs[1:]
    slots, tok, hidden = acts.shape
    columns = grads.shape[1]
    rows = grads.shape[0] // len(outs)
    row = lax.broadcasted_iota(jnp.int32, (tok, 1), 0)
    live = [jnp.where(row < counts[s], acts[s], jnp.zeros_like(acts[s])) for s in range(slots)]
    for k, out in enumerate(outs):
        start = pl.multiple_of((group[0] ^ k) * rows, CHUNK)
        out[:rows] = grads[pl.ds(start, rows)]
        for s in range(slots):
            for b in range(hidden // columns):
                to = rows + b * slots * tok + s * tok
                out[to : to + tok] = live[s][:, b * columns : (b + 1) * columns]


def pack_kernel(items, me, params, first, second, *refs):
    at = pl.program_id(0)
    for i, (j, _) in enumerate(items):

        @pl.when(at == i)
        def _(out=refs[-2:][j]):
            out[0] = params[...].astype(BF)
            out[1] = first[...]
            out[2] = second[...]


def bundle_kernel(picks, *refs):
    out, (buffer, came, went) = refs[-4], refs[-3:]
    arrive, leave = [], []
    for i, pick in enumerate(picks):
        ref = refs[i] if pick is None else refs[i].at[pick]
        arrive.append(pltpu.make_async_copy(ref, buffer.at[i], came.at[i]))
        leave.append(pltpu.make_async_copy(buffer.at[i], out.at[i], went.at[i]))
        arrive[i].start()
    for i in range(4):
        arrive[i].wait()
        leave[i].start()
    for i in range(4):
        leave[i].wait()


def grad_kernel(n, rows, me, *refs):
    at = pl.program_id(0)
    groups = lax.axis_size("edp")
    given, outs, table = refs[:groups], refs[-1 - n : -1], refs[-1]
    columns = given[0].shape[1]
    slots, piece, hidden = outs[0].shape
    tok = columns // slots

    @pl.when(at == 0)
    def _():
        table[...] = jnp.zeros_like(table)
        for g in range(groups):
            for b in range(hidden // columns):
                for s in range(slots):
                    source = rows + (b * slots + s) * tok
                    to, column = g * columns + s * tok, s * hidden + b * columns
                    table[to : to + tok, column : column + columns] = given[g][source : source + tok]

    here = pl.ds(pl.multiple_of((me[0] ^ at) * piece, CHUNK), piece)
    left = jnp.concatenate([given[g][here] for g in range(groups)], axis=1)
    total = jnp.dot(left, table[...], preferred_element_type=F32).astype(BF)
    for k in range(n):

        @pl.when(at == k)
        def _(k=k):
            for s in range(slots):
                outs[k][s] = total[:, s * hidden : (s + 1) * hidden]


def find(n, names, places):
    for e in range(n):
        places[names[e]] = e


def update_kernel(n, me_ref, old, rep, new, *refs):
    mine, outs = refs[:3], refs[-4 - n : -4]
    state, grads = refs[3 : 2 + n], dict(zip(ORDER, refs[2 + n : 2 + 2 * n]))
    sums, placed, owner, target = refs[-4:]
    me = me_ref[0]
    find(n, old, owner)
    find(n, new, target)
    to = [target[old[me ^ k]] ^ me for k in range(n)]
    serves = [owner[rep[me ^ k]] ^ me for k in range(n)]

    def update(r, _):
        rows = pl.ds(pl.multiple_of(r * CHUNK, CHUNK), CHUNK)
        for k in range(n):
            sums[k] = grads[k][0, rows].astype(F32)
        for k in range(n):
            sums[serves[k]] = sums[serves[k]] + grads[k][1, rows].astype(F32)
        for k in range(n):
            old_state = [ref[rows] for ref in mine] if k == 0 else [state[k - 1][i, rows] for i in range(3)]
            updated = quick_update(old_state[0].astype(F32), *old_state[1:], sums[k])
            for i, array in enumerate(updated):
                placed[to[k], i] = array.astype(BF)
        for k in range(n):
            outs[k][:, rows] = placed[k]
        return 0

    lax.fori_loop(0, mine[0].shape[0] // CHUNK, update, 0)


def unpack_kernel(begin, me_ref, *refs):
    (step, first, second), (given, wide, came, went) = refs[-7:-4], refs[-4:]
    me = me_ref[0]
    count, _, piece, width = given.shape
    pieces = refs[:count]

    def place(i):
        k = ORDER[i]
        row = pl.multiple_of((me ^ k) * piece, CHUNK)
        return pl.ds(row, piece), pl.ds(begin, width)

    arrive, leave = [], []
    for i in range(count):
        arrive.append(pltpu.make_async_copy(pieces[i], given.at[i], came.at[i]))
        arrive[-1].start()
    for i in range(count):
        arrive[i].wait()
        leave.append(pltpu.make_async_copy(given.at[i, 1], first.at[place(i)], went.at[3 * i]))
        leave.append(pltpu.make_async_copy(given.at[i, 2], second.at[place(i)], went.at[3 * i + 1]))
        leave[-2].start()
        leave[-1].start()
        wide[i] = given[i, 0].astype(F32)
        leave.append(pltpu.make_async_copy(wide.at[i], step.at[place(i)], went.at[3 * i + 2]))
        leave[-1].start()
    for copy in leave:
        copy.wait()


def bundle_kernel(*refs):
    out, (buffer, came, went) = refs[-4], refs[-3:]
    arrive, leave = [], []
    count = buffer.shape[0]
    for i in range(count):
        arrive.append(pltpu.make_async_copy(refs[i].at[min(i, 1)], buffer.at[i], came.at[i]))
        leave.append(pltpu.make_async_copy(buffer.at[i], out.at[i], went.at[i]))
        arrive[i].start()
    for i in range(count):
        arrive[i].wait()
        leave[i].start()
    for i in range(count):
        leave[i].wait()


def order_kernel(*refs):
    pass


def call(kernel, prefetch, grid, in_specs, out_specs, out_shape, scratch=(), aliases={}):
    return pl.pallas_call(
        kernel,
        grid_spec=pltpu.PrefetchScalarGridSpec(
            num_scalar_prefetch=prefetch,
            grid=grid,
            in_specs=in_specs,
            out_specs=out_specs,
            scratch_shapes=scratch,
        ),
        out_shape=out_shape,
        input_output_aliases=aliases,
        compiler_params=pltpu.CompilerParams(vmem_limit_bytes=LIMIT),
    )


def swap(array, k, axis):
    return lax.ppermute(array, axis, [(i, i ^ k) for i in range(lax.axis_size(axis))])


def fast_local(
    token_acts, out_grad, counts, params, first_moment, second_moment, old_expert, replica_of, new_expert
):
    groups = lax.axis_size("edp")
    n = lax.axis_size("ep")
    model_width, columns = out_grad.shape[2:]
    slots, tok, hidden = token_acts.shape[2:]
    rows = model_width // groups
    piece = rows // n
    unit = hidden // sum(SPLIT)
    block = min(FINE, unit)
    begins = [sum(SPLIT[:p]) * unit for p in range(len(SPLIT))]
    widths = [count * unit for count in SPLIT]
    me = lax.axis_index("ep").astype(jnp.int32).reshape(1)
    group = lax.axis_index("edp").astype(jnp.int32).reshape(1)
    params, first, second = params[0], first_moment[0], second_moment[0]
    whole = lambda *shape: pl.BlockSpec(shape, lambda i, *_: (0,) * len(shape))
    shape = lambda *dims: jax.ShapeDtypeStruct(dims, BF)
    hbm = pl.BlockSpec(memory_space=pltpu.HBM)
    others = ORDER[1:]

    def order(after, *arrays):
        return call(
            order_kernel,
            0,
            (),
            [hbm] * (len(arrays) + len(after)),
            [hbm] * len(arrays),
            [jax.ShapeDtypeStruct(array.shape, array.dtype) for array in arrays],
            aliases={j: j for j in range(len(arrays))},
        )(*arrays, *after)

    def pack(ks, counts, after):
        def source(i, me):
            k = ks[-1]
            for j in range(len(ks) - 1):
                k = jnp.where(i == j, ks[j], k)
            return (me[0] ^ k, 0)

        def slot(j):
            begin = sum(counts[:j])
            return pl.BlockSpec(
                (None, 3, piece, hidden), lambda i, *_: (jnp.clip(i - begin, 0, counts[j] - 1), 0, 0, 0)
            )

        items = [(j, s) for j in range(2) for s in range(counts[j])]
        return call(
            functools.partial(pack_kernel, items),
            1,
            (len(ks),),
            [pl.BlockSpec((piece, hidden), source)] * 3 + [hbm] * len(after),
            [slot(j) for j in range(2)],
            [shape(count, 3, piece, hidden) for count in counts],
        )(me, params, first, second, *after)

    sends = pack([4, 5, 2, 3], [2, 2], [])
    came = [swap(sends[1], 2, "ep"), swap(sends[0], 4, "ep")]

    tall = rows + slots * tok * (hidden // columns)
    spread = call(
        spread_kernel,
        2,
        (1,),
        [whole(model_width, columns), whole(slots, tok, hidden), hbm],
        [whole(tall, columns)] * groups,
        [shape(tall, columns)] * groups,
    )(group, counts[0, 0], out_grad[0, 0], token_acts[0, 0], sends[0])
    given = [spread[0]] + [swap(spread[k], k, "edp") for k in range(1, groups)]
    diagonal, near = pack([6, 7, 1], [2, 1], [spread[0]])
    came.append(swap(diagonal, 6, "ep"))

    made = call(
        functools.partial(grad_kernel, n, rows),
        1,
        (n,),
        [whole(tall, columns)] * groups,
        [whole(slots, piece, hidden)] * n,
        [shape(slots, piece, hidden)] * n,
        [pltpu.VMEM((groups * columns, slots * hidden), BF)],
    )(me, *given)
    grads = {0: made[0], **{k: swap(made[k], k, "ep") for k in others}}
    came = order([made[0]], *came)
    passed = swap(
        call(
            bundle_kernel,
            0,
            (),
            [hbm] * (4),
            hbm,
            shape(4, 3, piece, hidden),
            [
                pltpu.VMEM((4, 3, piece, hidden), BF),
                pltpu.SemaphoreType.DMA((4,)),
                pltpu.SemaphoreType.DMA((4,)),
            ],
        )(near, *came),
        1,
        "ep",
    )
    state = [(passed, 0)] + [part for j in range(3) for part in ((came[j], 0), (passed, 1 + j))]

    homes = []
    for p, (begin, width) in enumerate(zip(begins, widths)):
        first_block = begin // block
        mine = pl.BlockSpec((piece, block), lambda i, me, *_, at=first_block: (me[0], at + i))
        held = lambda slot, at=first_block: pl.BlockSpec((None, 3, piece, block), lambda i, *_: (slot, 0, 0, at + i))
        part = pl.BlockSpec((slots, piece, block), lambda i, *_, at=first_block: (0, 0, at + i))
        after = homes[-1][:1] if homes else []
        homes.append(
            call(
                functools.partial(update_kernel, n),
                4,
                (width // block,),
                [mine] * 3 + [held(slot) for _, slot in state] + [part] * n + [hbm] * len(after),
                [pl.BlockSpec((3, piece, block), lambda i, *_: (0, 0, i))] * n,
                [shape(3, piece, width)] * n,
                [
                    pltpu.VMEM((n, CHUNK, block), F32),
                    pltpu.VMEM((n, 3, CHUNK, block), BF),
                    pltpu.SMEM((n,), jnp.int32),
                    pltpu.SMEM((n,), jnp.int32),
                ],
            )(
                me, old_expert, replica_of, new_expert, params, first, second,
                *[array for array, _ in state], *[grads[k] for k in ORDER], *after,
            )
        )

    result = []
    for p, (begin, width) in enumerate(zip(begins, widths)):
        pieces = {0: homes[p][0], **{k: swap(homes[p][k], k, "ep") for k in others}}
        result = call(
            functools.partial(unpack_kernel, begin),
            1,
            (),
            [hbm] * (n + len(result)),
            [hbm] * 3,
            [jax.ShapeDtypeStruct((rows, hidden), d) for d in (F32, BF, BF)],
            [
                pltpu.VMEM((n, 3, piece, width), BF),
                pltpu.VMEM((n, piece, width), F32),
                pltpu.SemaphoreType.DMA((n,)),
                pltpu.SemaphoreType.DMA((3 * n,)),
            ],
            {1 + n + j: j for j in range(len(result))},
        )(me, *[pieces[k] for k in ORDER], *result)
    step, first, second = result
    return step[None], first[None], second[None]


def plain_local(
    token_acts, out_grad, counts, params, first_moment, second_moment, old_expert, replica_of, new_expert
):
    groups = lax.axis_size("edp")
    owners = lax.axis_size("ep")
    model_width = out_grad.shape[2]
    slots, tok, hidden = token_acts.shape[2:]
    rows = model_width // groups
    piece = rows * hidden // owners
    exchange = functools.partial(lax.all_to_all, axis_name="ep", split_axis=0, concat_axis=0, tiled=True)
    row = jnp.arange(tok, dtype=jnp.int32)
    live = row[None, :] < counts[0, 0][:, None]
    acts = jnp.where(live[:, :, None], token_acts[0, 0], jnp.zeros_like(token_acts[0, 0]))
    all_acts = lax.all_gather(acts, "edp", axis=0)
    all_grads = lax.all_to_all(
        out_grad[0, 0].reshape(groups, rows, slots * tok), "edp", split_axis=0, concat_axis=0, tiled=True
    ).reshape(groups, rows, slots, tok)
    slot_grads = jnp.einsum("adst,astf->sdf", all_grads, all_acts, preferred_element_type=F32)
    pieces = lambda array: exchange(array.astype(BF).reshape(owners, piece))
    own, replica = pieces(slot_grads[0]), pieces(slot_grads[1])
    sum_matrix = (replica_of[None, :] == old_expert[:, None]).astype(BF)
    move_matrix = (old_expert[None, :] == new_expert[:, None]).astype(BF)
    total = own.astype(F32) + jnp.dot(sum_matrix, replica, preferred_element_type=F32)
    updated = adam_update(
        pieces(params[0]).astype(F32), pieces(first_moment[0]), pieces(second_moment[0]), total
    )
    result = []
    for array, kind in zip(updated, (F32, BF, BF)):
        placed = jnp.dot(move_matrix, array.astype(BF), preferred_element_type=F32)
        result.append(exchange(placed.astype(BF)).astype(kind).reshape(1, rows, hidden))
    return tuple(result)


def local(token_acts, out_grad, *others):
    groups, n = lax.axis_size("edp"), lax.axis_size("ep")
    rows, columns = out_grad.shape[2] // groups, out_grad.shape[3]
    slots, tok, hidden = token_acts.shape[2:]
    fast = n == 8 and groups & (groups - 1) == 0 and rows % (8 * CHUNK) == 0
    fast = fast and slots == 2 and columns == 128 and tok == 64 and hidden % (FINE * sum(SPLIT)) == 0
    return (fast_local if fast else plain_local)(token_acts, out_grad, *others)


def solution(mesh):
    return jax.shard_map(
        local,
        mesh=mesh,
        in_specs=(
            P("edp", "ep", None, None, None),
            P("edp", "ep", None, None),
            P("edp", "ep", None),
            P("ep", "edp", None),
            P("ep", "edp", None),
            P("ep", "edp", None),
            P(),
            P(),
            P(),
        ),
        out_specs=(P("ep", "edp", None), P("ep", "edp", None), P("ep", "edp", None)),
        check_vma=False,
    )
```

```python
import functools

import jax
import jax.numpy as jnp
from jax import lax
from jax.experimental import pallas as pl
from jax.experimental.pallas import tpu as pltpu
from jax.sharding import PartitionSpec as P

beta_one = 0.9
beta_two = 0.95
bias_one = 0.9999734386011124
bias_two = 0.994079470779666
decay_rate = 0.1
adam_eps = 1e-08

BF = jnp.bfloat16
F32 = jnp.float32
CHUNK = 16
LIMIT = 56 * 1024 * 1024
FINE = 256
SPLIT = (2, 2)
ORDER = (0, 6, 2, 4, 3, 5, 7, 1)


def adam_update(weights, first_old, second_old, gradient):
    first_new = beta_one * first_old.astype(F32) + (1.0 - beta_one) * gradient
    second_new = beta_two * second_old.astype(F32) + (1.0 - beta_two) * gradient * gradient
    scaled = first_new / bias_one / (jnp.sqrt(second_new / bias_two) + adam_eps)
    step_new = -(scaled + decay_rate * weights)
    return step_new, first_new, second_new


def quick_update(weights, first_old, second_old, gradient):
    first_new = beta_one * first_old.astype(F32) + (1.0 - beta_one) * gradient
    second_new = beta_two * second_old.astype(F32) + (1.0 - beta_two) * gradient * gradient
    unbiased = second_new * (1.0 / bias_two)
    root = unbiased * lax.rsqrt(unbiased) + adam_eps
    scaled = first_new * (-1.0 / bias_one) * pl.reciprocal(root, approx=True)
    return scaled - decay_rate * weights, first_new, second_new


def spread_kernel(group, counts, grads, acts, *refs):
    outs = refs[1:]
    slots, tok, hidden = acts.shape
    columns = grads.shape[1]
    rows = grads.shape[0] // len(outs)
    row = lax.broadcasted_iota(jnp.int32, (tok, 1), 0)
    live = [jnp.where(row < counts[s], acts[s], jnp.zeros_like(acts[s])) for s in range(slots)]
    for k, out in enumerate(outs):
        start = pl.multiple_of((group[0] ^ k) * rows, CHUNK)
        out[:rows] = grads[pl.ds(start, rows)]
        for s in range(slots):
            for b in range(hidden // columns):
                to = rows + b * slots * tok + s * tok
                out[to : to + tok] = live[s][:, b * columns : (b + 1) * columns]


def pack_kernel(items, me, params, first, second, *refs):
    at = pl.program_id(0)
    for i, (j, _) in enumerate(items):

        @pl.when(at == i)
        def _(out=refs[-2:][j]):
            out[0] = params[...].astype(BF)
            out[1] = first[...]
            out[2] = second[...]


def bundle_kernel(picks, *refs):
    out, (buffer, came, went) = refs[-4], refs[-3:]
    arrive, leave = [], []
    for i, pick in enumerate(picks):
        ref = refs[i] if pick is None else refs[i].at[pick]
        arrive.append(pltpu.make_async_copy(ref, buffer.at[i], came.at[i]))
        leave.append(pltpu.make_async_copy(buffer.at[i], out.at[i], went.at[i]))
        arrive[i].start()
    for i in range(4):
        arrive[i].wait()
        leave[i].start()
    for i in range(4):
        leave[i].wait()


def grad_kernel(n, count, rows, me, *refs):
    at = pl.program_id(0)
    groups = lax.axis_size("edp")
    given, outs, table = refs[:groups], refs[-1 - n * count : -1], refs[-1]
    columns = given[0].shape[1]
    slots, piece, width = outs[0].shape
    hidden = width * count
    tok = columns // slots

    @pl.when(at == 0)
    def _():
        table[...] = jnp.zeros_like(table)
        for g in range(groups):
            for b in range(hidden // columns):
                for s in range(slots):
                    source = rows + (b * slots + s) * tok
                    to, column = g * columns + s * tok, s * hidden + b * columns
                    table[to : to + tok, column : column + columns] = given[g][source : source + tok]

    here = pl.ds(pl.multiple_of((me[0] ^ at) * piece, CHUNK), piece)
    left = jnp.concatenate([given[g][here] for g in range(groups)], axis=1)
    total = jnp.dot(left, table[...], preferred_element_type=F32).astype(BF)
    for k in range(n):

        @pl.when(at == k)
        def _(k=k):
            for s in range(slots):
                for p in range(count):
                    start = s * hidden + p * width
                    outs[p * n + k][s] = total[:, start : start + width]


def find(n, names, places):
    for e in range(n):
        places[names[e]] = e


def update_kernel(n, me_ref, old, rep, new, *refs):
    mine, outs = refs[:3], refs[-4 - n : -4]
    state, grads = refs[3 : 2 + n], dict(zip(ORDER, refs[2 + n : 2 + 2 * n]))
    sums, placed, owner, target = refs[-4:]
    me = me_ref[0]
    find(n, old, owner)
    find(n, new, target)
    to = [target[old[me ^ k]] ^ me for k in range(n)]
    serves = [owner[rep[me ^ k]] ^ me for k in range(n)]

    def update(r, _):
        rows = pl.ds(pl.multiple_of(r * CHUNK, CHUNK), CHUNK)
        for k in range(n):
            sums[k] = grads[k][0, rows].astype(F32)
        for k in range(n):
            sums[serves[k]] = sums[serves[k]] + grads[k][1, rows].astype(F32)
        for k in range(n):
            old_state = [ref[rows] for ref in mine] if k == 0 else [state[k - 1][i, rows] for i in range(3)]
            updated = quick_update(old_state[0].astype(F32), *old_state[1:], sums[k])
            for i, array in enumerate(updated):
                placed[to[k], i] = array.astype(BF)
        for k in range(n):
            outs[k][:, rows] = placed[k]
        return 0

    lax.fori_loop(0, mine[0].shape[0] // CHUNK, update, 0)


def unpack_kernel(begin, me_ref, *refs):
    (step, first, second), (given, wide, came, went) = refs[-7:-4], refs[-4:]
    me = me_ref[0]
    count, _, piece, width = given.shape
    pieces = refs[:count]

    def place(i):
        k = ORDER[i]
        row = pl.multiple_of((me ^ k) * piece, CHUNK)
        return pl.ds(row, piece), pl.ds(begin, width)

    arrive, leave = [], []
    for i in range(count):
        arrive.append(pltpu.make_async_copy(pieces[i], given.at[i], came.at[i]))
        arrive[-1].start()
    for i in range(count):
        arrive[i].wait()
        leave.append(pltpu.make_async_copy(given.at[i, 1], first.at[place(i)], went.at[3 * i]))
        leave.append(pltpu.make_async_copy(given.at[i, 2], second.at[place(i)], went.at[3 * i + 1]))
        leave[-2].start()
        leave[-1].start()
        wide[i] = given[i, 0].astype(F32)
        leave.append(pltpu.make_async_copy(wide.at[i], step.at[place(i)], went.at[3 * i + 2]))
        leave[-1].start()
    for copy in leave:
        copy.wait()


def bundle_kernel(*refs):
    out, (buffer, came, went) = refs[-4], refs[-3:]
    arrive, leave = [], []
    count = buffer.shape[0]
    for i in range(count):
        arrive.append(pltpu.make_async_copy(refs[i].at[min(i, 1)], buffer.at[i], came.at[i]))
        leave.append(pltpu.make_async_copy(buffer.at[i], out.at[i], went.at[i]))
        arrive[i].start()
    for i in range(count):
        arrive[i].wait()
        leave[i].start()
    for i in range(count):
        leave[i].wait()


def order_kernel(*refs):
    pass


def call(kernel, prefetch, grid, in_specs, out_specs, out_shape, scratch=(), aliases={}):
    return pl.pallas_call(
        kernel,
        grid_spec=pltpu.PrefetchScalarGridSpec(
            num_scalar_prefetch=prefetch,
            grid=grid,
            in_specs=in_specs,
            out_specs=out_specs,
            scratch_shapes=scratch,
        ),
        out_shape=out_shape,
        input_output_aliases=aliases,
        compiler_params=pltpu.CompilerParams(vmem_limit_bytes=LIMIT),
    )


def swap(array, k, axis):
    return lax.ppermute(array, axis, [(i, i ^ k) for i in range(lax.axis_size(axis))])


def fast_local(
    token_acts, out_grad, counts, params, first_moment, second_moment, old_expert, replica_of, new_expert
):
    groups = lax.axis_size("edp")
    n = lax.axis_size("ep")
    model_width, columns = out_grad.shape[2:]
    slots, tok, hidden = token_acts.shape[2:]
    rows = model_width // groups
    piece = rows // n
    unit = hidden // sum(SPLIT)
    block = min(FINE, unit)
    begins = [sum(SPLIT[:p]) * unit for p in range(len(SPLIT))]
    widths = [count * unit for count in SPLIT]
    me = lax.axis_index("ep").astype(jnp.int32).reshape(1)
    group = lax.axis_index("edp").astype(jnp.int32).reshape(1)
    params, first, second = params[0], first_moment[0], second_moment[0]
    whole = lambda *shape: pl.BlockSpec(shape, lambda i, *_: (0,) * len(shape))
    shape = lambda *dims: jax.ShapeDtypeStruct(dims, BF)
    hbm = pl.BlockSpec(memory_space=pltpu.HBM)
    others = ORDER[1:]

    def order(after, *arrays):
        return call(
            order_kernel,
            0,
            (),
            [hbm] * (len(arrays) + len(after)),
            [hbm] * len(arrays),
            [jax.ShapeDtypeStruct(array.shape, array.dtype) for array in arrays],
            aliases={j: j for j in range(len(arrays))},
        )(*arrays, *after)

    def pack(ks, counts, after):
        def source(i, me):
            k = ks[-1]
            for j in range(len(ks) - 1):
                k = jnp.where(i == j, ks[j], k)
            return (me[0] ^ k, 0)

        def slot(j):
            begin = sum(counts[:j])
            return pl.BlockSpec(
                (None, 3, piece, hidden), lambda i, *_: (jnp.clip(i - begin, 0, counts[j] - 1), 0, 0, 0)
            )

        items = [(j, s) for j in range(2) for s in range(counts[j])]
        return call(
            functools.partial(pack_kernel, items),
            1,
            (len(ks),),
            [pl.BlockSpec((piece, hidden), source)] * 3 + [hbm] * len(after),
            [slot(j) for j in range(2)],
            [shape(count, 3, piece, hidden) for count in counts],
        )(me, params, first, second, *after)

    sends = pack([4, 5, 2, 3], [2, 2], [])
    came = [swap(sends[1], 2, "ep"), swap(sends[0], 4, "ep")]

    tall = rows + slots * tok * (hidden // columns)
    spread = call(
        spread_kernel,
        2,
        (1,),
        [whole(model_width, columns), whole(slots, tok, hidden), hbm],
        [whole(tall, columns)] * groups,
        [shape(tall, columns)] * groups,
    )(group, counts[0, 0], out_grad[0, 0], token_acts[0, 0], sends[0])
    given = [spread[0]] + [swap(spread[k], k, "edp") for k in range(1, groups)]
    diagonal, near = pack([6, 7, 1], [2, 1], [spread[0]])
    came.append(swap(diagonal, 6, "ep"))

    count = len(SPLIT)
    made = call(
        functools.partial(grad_kernel, n, count, rows),
        1,
        (n,),
        [whole(tall, columns)] * groups,
        [whole(slots, piece, hidden // count)] * (n * count),
        [shape(slots, piece, hidden // count)] * (n * count),
        [pltpu.VMEM((groups * columns, slots * hidden), BF)],
    )(me, *given)
    all_grads = [
        {0: made[p * n], **{k: swap(made[p * n + k], k, "ep") for k in others}} for p in range(count)
    ]
    came = order([made[0]], *came)
    passed = swap(
        call(
            bundle_kernel,
            0,
            (),
            [hbm] * 4,
            hbm,
            shape(4, 3, piece, hidden),
            [
                pltpu.VMEM((4, 3, piece, hidden), BF),
                pltpu.SemaphoreType.DMA((4,)),
                pltpu.SemaphoreType.DMA((4,)),
            ],
        )(near, *came),
        1,
        "ep",
    )
    state = [(passed, 0)] + [part for j in range(3) for part in ((came[j], 0), (passed, 1 + j))]

    homes = []
    for p, (begin, width) in enumerate(zip(begins, widths)):
        first_block = begin // block
        grads = all_grads[p]
        mine = pl.BlockSpec((piece, block), lambda i, me, *_, at=first_block: (me[0], at + i))
        held = lambda slot, at=first_block: pl.BlockSpec((None, 3, piece, block), lambda i, *_: (slot, 0, 0, at + i))
        part = pl.BlockSpec((slots, piece, block), lambda i, *_: (0, 0, i))
        after = homes[-1][:1] if homes else []
        homes.append(
            call(
                functools.partial(update_kernel, n),
                4,
                (width // block,),
                [mine] * 3 + [held(slot) for _, slot in state] + [part] * n + [hbm] * len(after),
                [pl.BlockSpec((3, piece, block), lambda i, *_: (0, 0, i))] * n,
                [shape(3, piece, width)] * n,
                [
                    pltpu.VMEM((n, CHUNK, block), F32),
                    pltpu.VMEM((n, 3, CHUNK, block), BF),
                    pltpu.SMEM((n,), jnp.int32),
                    pltpu.SMEM((n,), jnp.int32),
                ],
            )(
                me, old_expert, replica_of, new_expert, params, first, second,
                *[array for array, _ in state], *[grads[k] for k in ORDER], *after,
            )
        )

    result = []
    for p, (begin, width) in enumerate(zip(begins, widths)):
        pieces = {0: homes[p][0], **{k: swap(homes[p][k], k, "ep") for k in others}}
        result = call(
            functools.partial(unpack_kernel, begin),
            1,
            (),
            [hbm] * (n + len(result)),
            [hbm] * 3,
            [jax.ShapeDtypeStruct((rows, hidden), d) for d in (F32, BF, BF)],
            [
                pltpu.VMEM((n, 3, piece, width), BF),
                pltpu.VMEM((n, piece, width), F32),
                pltpu.SemaphoreType.DMA((n,)),
                pltpu.SemaphoreType.DMA((3 * n,)),
            ],
            {1 + n + j: j for j in range(len(result))},
        )(me, *[pieces[k] for k in ORDER], *result)
    step, first, second = result
    return step[None], first[None], second[None]


def plain_local(
    token_acts, out_grad, counts, params, first_moment, second_moment, old_expert, replica_of, new_expert
):
    groups = lax.axis_size("edp")
    owners = lax.axis_size("ep")
    model_width = out_grad.shape[2]
    slots, tok, hidden = token_acts.shape[2:]
    rows = model_width // groups
    piece = rows * hidden // owners
    exchange = functools.partial(lax.all_to_all, axis_name="ep", split_axis=0, concat_axis=0, tiled=True)
    row = jnp.arange(tok, dtype=jnp.int32)
    live = row[None, :] < counts[0, 0][:, None]
    acts = jnp.where(live[:, :, None], token_acts[0, 0], jnp.zeros_like(token_acts[0, 0]))
    all_acts = lax.all_gather(acts, "edp", axis=0)
    all_grads = lax.all_to_all(
        out_grad[0, 0].reshape(groups, rows, slots * tok), "edp", split_axis=0, concat_axis=0, tiled=True
    ).reshape(groups, rows, slots, tok)
    slot_grads = jnp.einsum("adst,astf->sdf", all_grads, all_acts, preferred_element_type=F32)
    pieces = lambda array: exchange(array.astype(BF).reshape(owners, piece))
    own, replica = pieces(slot_grads[0]), pieces(slot_grads[1])
    sum_matrix = (replica_of[None, :] == old_expert[:, None]).astype(BF)
    move_matrix = (old_expert[None, :] == new_expert[:, None]).astype(BF)
    total = own.astype(F32) + jnp.dot(sum_matrix, replica, preferred_element_type=F32)
    updated = adam_update(
        pieces(params[0]).astype(F32), pieces(first_moment[0]), pieces(second_moment[0]), total
    )
    result = []
    for array, kind in zip(updated, (F32, BF, BF)):
        placed = jnp.dot(move_matrix, array.astype(BF), preferred_element_type=F32)
        result.append(exchange(placed.astype(BF)).astype(kind).reshape(1, rows, hidden))
    return tuple(result)


def local(token_acts, out_grad, *others):
    groups, n = lax.axis_size("edp"), lax.axis_size("ep")
    rows, columns = out_grad.shape[2] // groups, out_grad.shape[3]
    slots, tok, hidden = token_acts.shape[2:]
    fast = n == 8 and groups & (groups - 1) == 0 and rows % (8 * CHUNK) == 0
    fast = fast and len(set(SPLIT)) == 1 and slots == 2 and columns == 128 and tok == 64 and hidden % (FINE * sum(SPLIT)) == 0
    return (fast_local if fast else plain_local)(token_acts, out_grad, *others)


def solution(mesh):
    return jax.shard_map(
        local,
        mesh=mesh,
        in_specs=(
            P("edp", "ep", None, None, None),
            P("edp", "ep", None, None),
            P("edp", "ep", None),
            P("ep", "edp", None),
            P("ep", "edp", None),
            P("ep", "edp", None),
            P(),
            P(),
            P(),
        ),
        out_specs=(P("ep", "edp", None), P("ep", "edp", None), P("ep", "edp", None)),
        check_vma=False,
    )
```

```python
import functools

import jax
import jax.numpy as jnp
from jax import lax
from jax.experimental import pallas as pl
from jax.experimental.pallas import tpu as pltpu
from jax.sharding import PartitionSpec as P

beta_one = 0.9
beta_two = 0.95
bias_one = 0.9999734386011124
bias_two = 0.994079470779666
decay_rate = 0.1
adam_eps = 1e-08

BF = jnp.bfloat16
F32 = jnp.float32
CHUNK = 16
LIMIT = 61 * 1024 * 1024
FINE = 256
SPLIT = (2, 2)
ORDER = (0, 6, 2, 4, 3, 5, 7, 1)


def adam_update(weights, first_old, second_old, gradient):
    first_new = beta_one * first_old.astype(F32) + (1.0 - beta_one) * gradient
    second_new = beta_two * second_old.astype(F32) + (1.0 - beta_two) * gradient * gradient
    scaled = first_new / bias_one / (jnp.sqrt(second_new / bias_two) + adam_eps)
    step_new = -(scaled + decay_rate * weights)
    return step_new, first_new, second_new


def quick_update(weights, first_old, second_old, gradient):
    first_new = beta_one * first_old.astype(F32) + (1.0 - beta_one) * gradient
    second_new = beta_two * second_old.astype(F32) + (1.0 - beta_two) * gradient * gradient
    unbiased = second_new * (1.0 / bias_two)
    root = unbiased * lax.rsqrt(unbiased) + adam_eps
    scaled = first_new * (-1.0 / bias_one) * pl.reciprocal(root, approx=True)
    return scaled - decay_rate * weights, first_new, second_new


def spread_kernel(group, counts, grads, acts, *refs):
    outs = refs[1:]
    slots, tok, hidden = acts.shape
    columns = grads.shape[1]
    rows = grads.shape[0] // len(outs)
    row = lax.broadcasted_iota(jnp.int32, (tok, 1), 0)
    live = [jnp.where(row < counts[s], acts[s], jnp.zeros_like(acts[s])) for s in range(slots)]
    for k, out in enumerate(outs):
        start = pl.multiple_of((group[0] ^ k) * rows, CHUNK)
        out[:rows] = grads[pl.ds(start, rows)]
        for s in range(slots):
            for b in range(hidden // columns):
                to = rows + b * slots * tok + s * tok
                out[to : to + tok] = live[s][:, b * columns : (b + 1) * columns]


def pack_kernel(items, me, params, first, second, *refs):
    at = pl.program_id(0)
    for i, (j, _) in enumerate(items):

        @pl.when(at == i)
        def _(out=refs[-2:][j]):
            out[0] = params[...].astype(BF)
            out[1] = first[...]
            out[2] = second[...]


def bundle_kernel(picks, *refs):
    out, (buffer, came, went) = refs[-4], refs[-3:]
    arrive, leave = [], []
    for i, pick in enumerate(picks):
        ref = refs[i] if pick is None else refs[i].at[pick]
        arrive.append(pltpu.make_async_copy(ref, buffer.at[i], came.at[i]))
        leave.append(pltpu.make_async_copy(buffer.at[i], out.at[i], went.at[i]))
        arrive[i].start()
    for i in range(4):
        arrive[i].wait()
        leave[i].start()
    for i in range(4):
        leave[i].wait()


def grad_kernel(n, count, rows, me, *refs):
    at = pl.program_id(0)
    groups = lax.axis_size("edp")
    given, outs, table = refs[:groups], refs[-1 - n * count : -1], refs[-1]
    columns = given[0].shape[1]
    slots, piece, width = outs[0].shape
    hidden = width * count
    tok = columns // slots

    @pl.when(at == 0)
    def _():
        table[...] = jnp.zeros_like(table)
        for g in range(groups):
            for b in range(hidden // columns):
                for s in range(slots):
                    source = rows + (b * slots + s) * tok
                    to, column = g * columns + s * tok, s * hidden + b * columns
                    table[to : to + tok, column : column + columns] = given[g][source : source + tok]

    here = pl.ds(pl.multiple_of((me[0] ^ at) * piece, CHUNK), piece)
    left = jnp.concatenate([given[g][here] for g in range(groups)], axis=1)
    total = jnp.dot(left, table[...], preferred_element_type=F32).astype(BF)
    for k in range(n):

        @pl.when(at == k)
        def _(k=k):
            for s in range(slots):
                for p in range(count):
                    start = s * hidden + p * width
                    outs[p * n + k][s] = total[:, start : start + width]


def find(n, names, places):
    for e in range(n):
        places[names[e]] = e


def update_kernel(n, me_ref, old, rep, new, *refs):
    mine, outs = refs[:3], refs[-4 - n : -4]
    state, grads = refs[3 : 2 + n], dict(zip(ORDER, refs[2 + n : 2 + 2 * n]))
    sums, placed, owner, target = refs[-4:]
    me = me_ref[0]
    find(n, old, owner)
    find(n, new, target)
    to = [target[old[me ^ k]] ^ me for k in range(n)]
    serves = [owner[rep[me ^ k]] ^ me for k in range(n)]

    def update(r, _):
        rows = pl.ds(pl.multiple_of(r * CHUNK, CHUNK), CHUNK)
        for k in range(n):
            sums[k] = grads[k][0, rows].astype(F32)
        for k in range(n):
            sums[serves[k]] = sums[serves[k]] + grads[k][1, rows].astype(F32)
        for k in range(n):
            old_state = [ref[rows] for ref in mine] if k == 0 else [state[k - 1][i, rows] for i in range(3)]
            updated = quick_update(old_state[0].astype(F32), *old_state[1:], sums[k])
            for i, array in enumerate(updated):
                placed[to[k], i] = array.astype(BF)
        for k in range(n):
            outs[k][:, rows] = placed[k]
        return 0

    lax.fori_loop(0, mine[0].shape[0] // CHUNK, update, 0)


def unpack_kernel(begin, me_ref, *refs):
    (step, first, second), (given, wide, came, went) = refs[-7:-4], refs[-4:]
    me = me_ref[0]
    count, _, piece, width = given.shape
    pieces = refs[:count]

    def place(i):
        k = ORDER[i]
        row = pl.multiple_of((me ^ k) * piece, CHUNK)
        return pl.ds(row, piece), pl.ds(begin, width)

    arrive, leave = [], []
    for i in range(count):
        arrive.append(pltpu.make_async_copy(pieces[i], given.at[i], came.at[i]))
        arrive[-1].start()
    for i in range(count):
        arrive[i].wait()
        leave.append(pltpu.make_async_copy(given.at[i, 1], first.at[place(i)], went.at[3 * i]))
        leave.append(pltpu.make_async_copy(given.at[i, 2], second.at[place(i)], went.at[3 * i + 1]))
        leave[-2].start()
        leave[-1].start()
        wide[i] = given[i, 0].astype(F32)
        leave.append(pltpu.make_async_copy(wide.at[i], step.at[place(i)], went.at[3 * i + 2]))
        leave[-1].start()
    for copy in leave:
        copy.wait()


def bundle_kernel(*refs):
    out, (buffer, came, went) = refs[-4], refs[-3:]
    arrive, leave = [], []
    count = buffer.shape[0]
    for i in range(count):
        arrive.append(pltpu.make_async_copy(refs[i].at[min(i, 1)], buffer.at[i], came.at[i]))
        leave.append(pltpu.make_async_copy(buffer.at[i], out.at[i], went.at[i]))
        arrive[i].start()
    for i in range(count):
        arrive[i].wait()
        leave[i].start()
    for i in range(count):
        leave[i].wait()


def order_kernel(*refs):
    pass


def call(kernel, prefetch, grid, in_specs, out_specs, out_shape, scratch=(), aliases={}):
    return pl.pallas_call(
        kernel,
        grid_spec=pltpu.PrefetchScalarGridSpec(
            num_scalar_prefetch=prefetch,
            grid=grid,
            in_specs=in_specs,
            out_specs=out_specs,
            scratch_shapes=scratch,
        ),
        out_shape=out_shape,
        input_output_aliases=aliases,
        compiler_params=pltpu.CompilerParams(vmem_limit_bytes=LIMIT),
    )


def swap(array, k, axis):
    return lax.ppermute(array, axis, [(i, i ^ k) for i in range(lax.axis_size(axis))])


def fast_local(
    token_acts, out_grad, counts, params, first_moment, second_moment, old_expert, replica_of, new_expert
):
    groups = lax.axis_size("edp")
    n = lax.axis_size("ep")
    model_width, columns = out_grad.shape[2:]
    slots, tok, hidden = token_acts.shape[2:]
    rows = model_width // groups
    piece = rows // n
    unit = hidden // sum(SPLIT)
    block = min(FINE, unit)
    begins = [sum(SPLIT[:p]) * unit for p in range(len(SPLIT))]
    widths = [count * unit for count in SPLIT]
    me = lax.axis_index("ep").astype(jnp.int32).reshape(1)
    group = lax.axis_index("edp").astype(jnp.int32).reshape(1)
    params, first, second = params[0], first_moment[0], second_moment[0]
    whole = lambda *shape: pl.BlockSpec(shape, lambda i, *_: (0,) * len(shape))
    shape = lambda *dims: jax.ShapeDtypeStruct(dims, BF)
    hbm = pl.BlockSpec(memory_space=pltpu.HBM)
    others = ORDER[1:]

    def order(after, *arrays):
        return call(
            order_kernel,
            0,
            (),
            [hbm] * (len(arrays) + len(after)),
            [hbm] * len(arrays),
            [jax.ShapeDtypeStruct(array.shape, array.dtype) for array in arrays],
            aliases={j: j for j in range(len(arrays))},
        )(*arrays, *after)

    def pack(ks, counts, after):
        def source(i, me):
            k = ks[-1]
            for j in range(len(ks) - 1):
                k = jnp.where(i == j, ks[j], k)
            return (me[0] ^ k, 0)

        def slot(j):
            begin = sum(counts[:j])
            return pl.BlockSpec(
                (None, 3, piece, hidden), lambda i, *_: (jnp.clip(i - begin, 0, counts[j] - 1), 0, 0, 0)
            )

        items = [(j, s) for j in range(2) for s in range(counts[j])]
        return call(
            functools.partial(pack_kernel, items),
            1,
            (len(ks),),
            [pl.BlockSpec((piece, hidden), source)] * 3 + [hbm] * len(after),
            [slot(j) for j in range(2)],
            [shape(count, 3, piece, hidden) for count in counts],
        )(me, params, first, second, *after)

    sends = pack([4, 5, 2, 3], [2, 2], [])
    came = [swap(sends[1], 2, "ep"), swap(sends[0], 4, "ep")]

    tall = rows + slots * tok * (hidden // columns)
    spread = call(
        spread_kernel,
        2,
        (1,),
        [whole(model_width, columns), whole(slots, tok, hidden), hbm],
        [whole(tall, columns)] * groups,
        [shape(tall, columns)] * groups,
    )(group, counts[0, 0], out_grad[0, 0], token_acts[0, 0], sends[0])
    given = [spread[0]] + [swap(spread[k], k, "edp") for k in range(1, groups)]
    diagonal, near = pack([6, 7, 1], [2, 1], [spread[0]])
    came.append(swap(diagonal, 6, "ep"))

    count = len(SPLIT)
    made = call(
        functools.partial(grad_kernel, n, count, rows),
        1,
        (n,),
        [whole(tall, columns)] * groups,
        [whole(slots, piece, hidden // count)] * (n * count),
        [shape(slots, piece, hidden // count)] * (n * count),
        [pltpu.VMEM((groups * columns, slots * hidden), BF)],
    )(me, *given)
    all_grads = [
        {0: made[p * n], **{k: swap(made[p * n + k], k, "ep") for k in others}} for p in range(count)
    ]
    came = order([made[0]], *came)
    passed = swap(
        call(
            bundle_kernel,
            0,
            (),
            [hbm] * 4,
            hbm,
            shape(4, 3, piece, hidden),
            [
                pltpu.VMEM((4, 3, piece, hidden), BF),
                pltpu.SemaphoreType.DMA((4,)),
                pltpu.SemaphoreType.DMA((4,)),
            ],
        )(near, *came),
        1,
        "ep",
    )
    state = [(passed, 0)] + [part for j in range(3) for part in ((came[j], 0), (passed, 1 + j))]

    homes = []
    for p, (begin, width) in enumerate(zip(begins, widths)):
        first_block = begin // block
        grads = all_grads[p]
        mine = pl.BlockSpec((piece, block), lambda i, me, *_, at=first_block: (me[0], at + i))
        held = lambda slot, at=first_block: pl.BlockSpec((None, 3, piece, block), lambda i, *_: (slot, 0, 0, at + i))
        part = pl.BlockSpec((slots, piece, block), lambda i, *_: (0, 0, i))
        after = homes[-1][:1] if homes else []
        homes.append(
            call(
                functools.partial(update_kernel, n),
                4,
                (width // block,),
                [mine] * 3 + [held(slot) for _, slot in state] + [part] * n + [hbm] * len(after),
                [pl.BlockSpec((3, piece, block), lambda i, *_: (0, 0, i))] * n,
                [shape(3, piece, width)] * n,
                [
                    pltpu.VMEM((n, CHUNK, block), F32),
                    pltpu.VMEM((n, 3, CHUNK, block), BF),
                    pltpu.SMEM((n,), jnp.int32),
                    pltpu.SMEM((n,), jnp.int32),
                ],
            )(
                me, old_expert, replica_of, new_expert, params, first, second,
                *[array for array, _ in state], *[grads[k] for k in ORDER], *after,
            )
        )

    result = []
    for p, (begin, width) in enumerate(zip(begins, widths)):
        pieces = {0: homes[p][0], **{k: swap(homes[p][k], k, "ep") for k in others}}
        result = call(
            functools.partial(unpack_kernel, begin),
            1,
            (),
            [hbm] * (n + len(result)),
            [hbm] * 3,
            [jax.ShapeDtypeStruct((rows, hidden), d) for d in (F32, BF, BF)],
            [
                pltpu.VMEM((n, 3, piece, width), BF),
                pltpu.VMEM((n, piece, width), F32),
                pltpu.SemaphoreType.DMA((n,)),
                pltpu.SemaphoreType.DMA((3 * n,)),
            ],
            {1 + n + j: j for j in range(len(result))},
        )(me, *[pieces[k] for k in ORDER], *result)
    step, first, second = result
    return step[None], first[None], second[None]


def plain_local(
    token_acts, out_grad, counts, params, first_moment, second_moment, old_expert, replica_of, new_expert
):
    groups = lax.axis_size("edp")
    owners = lax.axis_size("ep")
    model_width = out_grad.shape[2]
    slots, tok, hidden = token_acts.shape[2:]
    rows = model_width // groups
    piece = rows * hidden // owners
    exchange = functools.partial(lax.all_to_all, axis_name="ep", split_axis=0, concat_axis=0, tiled=True)
    row = jnp.arange(tok, dtype=jnp.int32)
    live = row[None, :] < counts[0, 0][:, None]
    acts = jnp.where(live[:, :, None], token_acts[0, 0], jnp.zeros_like(token_acts[0, 0]))
    all_acts = lax.all_gather(acts, "edp", axis=0)
    all_grads = lax.all_to_all(
        out_grad[0, 0].reshape(groups, rows, slots * tok), "edp", split_axis=0, concat_axis=0, tiled=True
    ).reshape(groups, rows, slots, tok)
    slot_grads = jnp.einsum("adst,astf->sdf", all_grads, all_acts, preferred_element_type=F32)
    pieces = lambda array: exchange(array.astype(BF).reshape(owners, piece))
    own, replica = pieces(slot_grads[0]), pieces(slot_grads[1])
    sum_matrix = (replica_of[None, :] == old_expert[:, None]).astype(BF)
    move_matrix = (old_expert[None, :] == new_expert[:, None]).astype(BF)
    total = own.astype(F32) + jnp.dot(sum_matrix, replica, preferred_element_type=F32)
    updated = adam_update(
        pieces(params[0]).astype(F32), pieces(first_moment[0]), pieces(second_moment[0]), total
    )
    result = []
    for array, kind in zip(updated, (F32, BF, BF)):
        placed = jnp.dot(move_matrix, array.astype(BF), preferred_element_type=F32)
        result.append(exchange(placed.astype(BF)).astype(kind).reshape(1, rows, hidden))
    return tuple(result)


def local(token_acts, out_grad, *others):
    groups, n = lax.axis_size("edp"), lax.axis_size("ep")
    rows, columns = out_grad.shape[2] // groups, out_grad.shape[3]
    slots, tok, hidden = token_acts.shape[2:]
    fast = n == 8 and groups & (groups - 1) == 0 and rows % (8 * CHUNK) == 0
    fast = fast and len(set(SPLIT)) == 1 and slots == 2 and columns == 128 and tok == 64 and hidden % (FINE * sum(SPLIT)) == 0
    return (fast_local if fast else plain_local)(token_acts, out_grad, *others)


def solution(mesh):
    return jax.shard_map(
        local,
        mesh=mesh,
        in_specs=(
            P("edp", "ep", None, None, None),
            P("edp", "ep", None, None),
            P("edp", "ep", None),
            P("ep", "edp", None),
            P("ep", "edp", None),
            P("ep", "edp", None),
            P(),
            P(),
            P(),
        ),
        out_specs=(P("ep", "edp", None), P("ep", "edp", None), P("ep", "edp", None)),
        check_vma=False,
    )
```
